32 devices in a mesh: section: 4 (over z), dp: 4 (over y, x), tensor: 2 (over core).
Axes of the slice: x: 2, y: 2, z: 4, core: 2. Of those that a mesh axis runs over, the one named last changes fastest.
Arguments:
- tokens: bfloat16 [4, 512, 4096], P('section', 'dp', 'tensor'), may hold values from -6 to 6
- lengths: int32 [4, 4], P(None, 'dp'), may hold values from 16 to 128, as said below
- w_query: bfloat16 [4, 4096, 256], P('section', None, 'tensor')
- w_key: bfloat16 [4, 4096, 256], P('section', None, 'tensor')
- w_value: bfloat16 [4, 4096, 256], P('section', None, 'tensor'), may hold values from -0.09375 to 0.09375
- w_out: bfloat16 [4, 256, 4096], P('section', 'tensor'), may hold values from -0.375 to 0.375
- w_embed: bfloat16 [4096, 1024], P('tensor'), may hold values from -0.09375 to 0.09375
Outputs:
- penalty_grad: float32 [4, 512, 1024], P('section', 'dp', 'tensor')
The draws below stay inside these ranges and needn't reach their ends.
Inputs may be any that keep to these rules, and one draw needn't show every extreme that they name: `lengths`: every length is at least 16; at least one length equals 128.
All inputs are finite; a program needn't handle non-finite values.
Results may differ from the reference program's by a relative error of at most 0.02.
Values may be sent and summed in bfloat16 or wider, within the bound.
No kernel may reach another device: no remote copies, remote signals or barrier semaphores. Data moves between devices by JAX's collectives and lax.ppermute only.
A program may use at most 64 MiB of HBM per device.

```python
import math
import jax
import jax.numpy as jnp
from jax import lax

D = 4096
HD = 128
HEADS = 2
E = 1024
HOPS = 2
SEQ = 128
SECTIONS = 4
GROUPS = 4
ROWS = 512
HW = 256
N_TENSOR = 2


def query_key_pair(key):
    shape = (SECTIONS, D, HW)
    base_key = jax.random.normal(jax.random.fold_in(key, 11), shape, jnp.float32) / jnp.sqrt(jnp.float32(D))
    base_query = jax.random.normal(jax.random.fold_in(key, 12), shape, jnp.float32) / jnp.sqrt(jnp.float32(D))
    queries = base_query
    return (queries, base_key)


def draw_w_query(key, part):
    return query_key_pair(key)[0].astype(jnp.bfloat16)


def draw_w_key(key, part):
    return query_key_pair(key)[1].astype(jnp.bfloat16)


def draw_lengths(key, part):
    drawn = jax.random.randint(jax.random.fold_in(key, 21), (SECTIONS * GROUPS,), SEQ // 8, SEQ + 1)
    chosen = jax.random.randint(jax.random.fold_in(key, 22), (), 0, SECTIONS * GROUPS)
    flat = jnp.where(jnp.arange(SECTIONS * GROUPS) == chosen, SEQ, drawn)
    return flat.reshape(SECTIONS, GROUPS).astype(jnp.int32)


def levels(rng, dims, cuts, low, top_value):
    level, own = 1.0, jax.random.fold_in(rng, 6)
    for axis_at, shards_of in cuts:
        draws = jnp.exp(jax.random.uniform(jax.random.fold_in(own, axis_at), (shards_of,), jnp.float32, low / len(cuts), top_value / len(cuts)))
        level = level * jnp.repeat(draws, dims[axis_at] // shards_of).reshape([-1 if axis == axis_at else 1 for axis in range(len(dims))])
    return level


def bell_draw(rng, extent, deviation, bound, cuts=(), kind=jnp.bfloat16):
    values = deviation * jax.random.normal(rng, extent, jnp.float32)
    if cuts:
        values = values * levels(rng, extent, cuts, -0.22, 0.18)
    return jnp.clip(values, -bound, bound).astype(kind)


def setup_inputs(seed: int = 0) -> dict:
    arg_keys = jax.random.split(jax.random.key(seed), 8)
    tokens = bell_draw(arg_keys[0], (SECTIONS, ROWS, D), 1.0, 6.0, ((0, 4), (1, 4), (2, 2)))
    lengths = draw_lengths(jax.random.fold_in(arg_keys[7], 71), 0)
    w_query = draw_w_query(jax.random.fold_in(arg_keys[7], 71), 0)
    w_key = draw_w_key(jax.random.fold_in(arg_keys[7], 71), 0)
    w_value = bell_draw(arg_keys[4], (SECTIONS, D, HW), D ** -0.5, 0.09375, ((0, 4), (2, 2)))
    w_out = bell_draw(arg_keys[5], (SECTIONS, HW, D), HW ** -0.5, 0.375, ((0, 4), (1, 2)))
    w_embed = bell_draw(arg_keys[6], (D, E), D ** -0.5, 0.09375, ((0, 2),))
    return {"tokens": tokens, "lengths": lengths, "w_query": w_query, "w_key": w_key, "w_value": w_value, "w_out": w_out, "w_embed": w_embed}


EPSILON = 1e-05

def layer_step(state, w_query, w_key, w_value, w_out, group_lens):
    values32 = state.astype(jnp.float32)
    normed = (values32 * lax.rsqrt(lax.optimization_barrier(jnp.mean(values32 * values32, axis=-1, keepdims=True)) + EPSILON)).astype(jnp.bfloat16)
    query_rows = jnp.dot(normed, w_query, preferred_element_type=jnp.float32).astype(jnp.bfloat16)
    key_rows = jnp.dot(normed, w_key, preferred_element_type=jnp.float32).astype(jnp.bfloat16)
    value_rows = jnp.dot(normed, w_value, preferred_element_type=jnp.float32).astype(jnp.bfloat16)
    query_h = query_rows.reshape(GROUPS, SEQ, HEADS, HD).astype(jnp.float32)
    key_h = key_rows.reshape(GROUPS, SEQ, HEADS, HD).astype(jnp.float32)
    value_h = value_rows.reshape(GROUPS, SEQ, HEADS, HD).astype(jnp.float32)
    scores = jnp.einsum('gqhd,gkhd->ghqk', query_h, key_h) * (1.0 / math.sqrt(HD))
    positions = jnp.arange(SEQ, dtype=jnp.int32)
    key_mask = positions[None, None, None, :] < group_lens[:, None, None, None]
    scores = jnp.where(key_mask, scores, -1e+30)
    row_max = lax.optimization_barrier(jnp.max(scores, axis=-1, keepdims=True))
    exp_scores = jnp.exp(scores - row_max)
    attn_probs = (exp_scores / lax.optimization_barrier(jnp.sum(exp_scores, axis=-1, keepdims=True))).astype(jnp.bfloat16)
    mixed = jnp.einsum('ghqk,gkhd->gqhd', attn_probs.astype(jnp.float32), value_h).astype(jnp.bfloat16)
    mixed = mixed.reshape(ROWS, HW)
    group_width = HW // N_TENSOR
    total = jnp.zeros((ROWS, D), jnp.float32)
    for core in range(N_TENSOR):
        lower = core * group_width
        part = jnp.dot(mixed[:, lower:lower + group_width], w_out[lower:lower + group_width], preferred_element_type=jnp.float32)
        total = total + part.astype(jnp.bfloat16).astype(jnp.float32)
    return (values32 + total).astype(jnp.bfloat16)

def reference(tokens, lengths, w_query, w_key, w_value, w_out, w_embed):

    def one_section(dest):
        anchor = (dest - (HOPS - 1)) % SECTIONS
        state = lax.dynamic_index_in_dim(tokens, anchor, 0, keepdims=False)
        group_lens = lax.dynamic_index_in_dim(lengths, anchor, 0, keepdims=False)
        for hop in range(HOPS):
            section_now = (anchor + hop) % SECTIONS
            state = layer_step(state, lax.dynamic_index_in_dim(w_query, section_now, 0, keepdims=False), lax.dynamic_index_in_dim(w_key, section_now, 0, keepdims=False), lax.dynamic_index_in_dim(w_value, section_now, 0, keepdims=False), lax.dynamic_index_in_dim(w_out, section_now, 0, keepdims=False), group_lens)
        feature_width = D // N_TENSOR
        total = jnp.zeros((ROWS, E), jnp.float32)
        for core in range(N_TENSOR):
            lower = core * feature_width
            part = jnp.dot(state[:, lower:lower + feature_width], w_embed[lower:lower + feature_width], preferred_element_type=jnp.float32)
            total = total + part.astype(jnp.bfloat16).astype(jnp.float32)
        embed = total.astype(jnp.bfloat16)
        positions = jnp.arange(SEQ, dtype=jnp.int32)
        row_live = (positions[None, :] < group_lens[:, None]).reshape(ROWS)
        masked = jnp.where(row_live[:, None], embed, jnp.zeros_like(embed))
        grouped = masked.reshape(GROUPS, SEQ, E).astype(jnp.float32)
        partials = jnp.einsum('gse,gsf->gef', grouped, grouped) / float(SEQ * GROUPS)
        moments = lax.optimization_barrier(jnp.sum(partials.astype(jnp.bfloat16).astype(jnp.float32), axis=0))
        penalty = (moments - jnp.eye(E, dtype=jnp.float32)).astype(jnp.bfloat16)
        return jnp.dot(masked, penalty, preferred_element_type=jnp.float32)
    return lax.map(one_section, jnp.arange(SECTIONS, dtype=jnp.int32))
```

```python
import functools
import math

import jax
import jax.numpy as jnp
from jax import lax
from jax.experimental import pallas as pl
from jax.experimental.pallas import tpu as pltpu
from jax.sharding import PartitionSpec as P

HD = 128
HOPS = 2
EPSILON = 1e-05
BF16 = jnp.bfloat16
F32 = jnp.float32
VMEM_BYTES = 16 * 1024 * 1024


def shifted(value, axis, steps):
    count = lax.axis_size(axis)
    pairs = [(source, (source + steps) % count) for source in range(count)]
    return lax.ppermute(value, axis, pairs)


def exchanged(value, axis, mask):
    count = lax.axis_size(axis)
    return lax.ppermute(value, axis, [(source, source ^ mask) for source in range(count)])


def dot(left, right):
    return lax.dot_general(left, right, (((1,), (0,)), ((), ())), preferred_element_type=F32)


def dot_t(left, right):
    return lax.dot_general(left, right, (((1,), (1,)), ((), ())), preferred_element_type=F32)


def call(body, out_shapes, n_smem, n_vmem, flops, scratch=()):
    return pl.pallas_call(
        body,
        out_shape=out_shapes,
        in_specs=[pl.BlockSpec(memory_space=pltpu.SMEM)] * n_smem
        + [pl.BlockSpec(memory_space=pltpu.VMEM)] * n_vmem,
        out_specs=jax.tree.map(lambda _: pl.BlockSpec(memory_space=pltpu.VMEM), out_shapes),
        scratch_shapes=scratch,
        compiler_params=pltpu.CompilerParams(vmem_limit_bytes=VMEM_BYTES),
        cost_estimate=pl.CostEstimate(flops=flops, bytes_accessed=2_000_000, transcendentals=0),
    )


def softmax_mix(query, key, value, live_len):
    rows = query.shape[0]
    scores = dot_t(query, key) * (1.0 / math.sqrt(HD))
    key_pos = lax.broadcasted_iota(jnp.int32, (rows, rows), 1)
    scores = jnp.where(key_pos < live_len, scores, -1e30)
    weights = jnp.exp(scores - jnp.max(scores, axis=-1, keepdims=True))
    probs = (weights / jnp.sum(weights, axis=-1, keepdims=True)).astype(BF16)
    return dot(probs, value).astype(BF16)


def project(state_refs, row_starts, w_refs, width, block):
    wq_ref, wk_ref, wv_ref = w_refs
    rows = state_refs[0].shape[0]
    qk = jnp.zeros((rows, 2 * HD), F32)
    val = jnp.zeros((rows, HD), F32)
    square = jnp.zeros((rows, HD), F32)
    for state_ref, row_start in zip(state_refs, row_starts):
        for at in range(0, width, block):
            x = state_ref[:, at : at + block]
            src = pl.ds(pl.multiple_of(row_start + at, block), block)
            qk += dot(x, jnp.concatenate([wq_ref[src, :], wk_ref[src, :]], axis=1))
            val += dot(x, wv_ref[src, :])
            x32 = x.astype(F32)
            x2 = x32 * x32
            for lane in range(0, block, HD):
                square += x2[:, lane : lane + HD]
    return qk, val, square


def attend(parts, row_starts, w_refs, live_len, width, block):
    qk, val, square = project(parts, row_starts, w_refs, width, block)
    features = w_refs[0].shape[0]
    scale = lax.rsqrt(jnp.sum(square, axis=-1, keepdims=True) * (1.0 / features) + EPSILON)
    query = (qk[:, :HD] * scale).astype(BF16)
    key = (qk[:, HD:] * scale).astype(BF16)
    value = (val * scale).astype(BF16)
    return softmax_mix(query, key, value, live_len)


def first_body(place_ref, own_ref, oth_ref, wq_ref, wk_ref, wv_ref, mixed_ref):
    half = own_ref.shape[1]
    core = place_ref[0]
    mixed_ref[...] = attend(
        [own_ref, oth_ref],
        [core * half, (1 - core) * half],
        (wq_ref, wk_ref, wv_ref),
        place_ref[1],
        half,
        512,
    )


def update_body(pieces, place_ref, own_ref, mix_own_ref, mix_oth_ref, w_own_ref, w_oth_ref, *outs):
    half = own_ref.shape[1]
    core = place_ref[0]
    width = half // pieces
    mixed = jnp.concatenate([mix_own_ref[...], mix_oth_ref[...]], axis=1)
    for piece in range(pieces):
        lower = piece * width
        cols = pl.ds(pl.multiple_of(core * half + lower, width), width)
        weight = jnp.concatenate([w_own_ref[:, cols], w_oth_ref[:, cols]], axis=0)
        held = own_ref[:, lower : lower + width].astype(F32)
        outs[piece][...] = (held + dot(mixed, weight)).astype(BF16)


def combine_body(place_ref, w_own_ref, w_oth_ref, e_own_ref, e_oth_ref, out_ref):
    half = e_own_ref.shape[0]
    cols_half = out_ref.shape[1]
    core = place_ref[0]
    cols = pl.ds(pl.multiple_of(core * cols_half, cols_half), cols_half)
    total = jnp.zeros(out_ref.shape, F32)
    block = 512
    for e_ref, start in ((e_own_ref, core * half), (e_oth_ref, (1 - core) * half)):
        for at in range(0, half, block):
            src = pl.ds(pl.multiple_of(start + at, block), block)
            weight = jnp.concatenate([w_own_ref[:, src], w_oth_ref[:, src]], axis=0)
            total += dot(weight, e_ref[at : at + block, cols])
    out_ref[...] = total.astype(BF16)


def second_body(pieces, place_ref, *refs):
    owns, oths = refs[:pieces], refs[pieces : 2 * pieces]
    wq_ref, wk_ref, wv_ref, e_own_ref, e_oth_ref, mixed_ref, embed_ref = refs[2 * pieces :]
    half = e_own_ref.shape[0]
    width = half // pieces
    core = place_ref[0]
    starts = [core * half + piece * width for piece in range(pieces)]
    starts += [(1 - core) * half + piece * width for piece in range(pieces)]
    mixed_ref[...] = attend(
        list(owns) + list(oths), starts, (wq_ref, wk_ref, wv_ref), place_ref[2], width, 512
    )
    cols_half = embed_ref.shape[1]
    cols = pl.ds(pl.multiple_of(core * cols_half, cols_half), cols_half)
    total = jnp.zeros(embed_ref.shape, F32)
    for e_ref, parts in ((e_own_ref, owns), (e_oth_ref, oths)):
        for piece in range(pieces):
            total += dot(parts[piece][...], e_ref[piece * width : (piece + 1) * width, cols])
    embed_ref[...] = total


def embed_body(place_ref, embed_ref, mix_own_ref, mix_oth_ref, combined_ref, out_ref):
    rows = out_ref.shape[0]
    mixed = jnp.concatenate([mix_own_ref[...], mix_oth_ref[...]], axis=1)
    embed = embed_ref[...] + dot(mixed, combined_ref[...])
    row_pos = lax.broadcasted_iota(jnp.int32, embed.shape, 0)
    out_ref[...] = jnp.where(row_pos < place_ref[2], embed, 0.0).astype(BF16)


def gram_body(*refs):
    embeds, out_ref = refs[:-1], refs[-1]
    rows = embeds[0].shape[0]
    own = embeds[0][...]
    for at, other in enumerate(embeds):
        out_ref[:, at * rows : (at + 1) * rows] = dot_t(own, other[...])


def result_body(*refs):
    embeds, (gram_own_ref, gram_oth_ref, out_ref) = refs[:-3], refs[-3:]
    rows = embeds[0].shape[0]
    tokens = rows * len(embeds)
    total = jnp.zeros(out_ref.shape, F32)
    for at, embed in enumerate(embeds):
        cols = slice(at * rows, (at + 1) * rows)
        gram = (gram_own_ref[:, cols] + gram_oth_ref[:, cols]) * (1.0 / tokens)
        if at == 0:
            row = lax.broadcasted_iota(jnp.int32, gram.shape, 0)
            col = lax.broadcasted_iota(jnp.int32, gram.shape, 1)
            gram = gram - (row == col).astype(F32)
        total += dot(gram.astype(BF16), embed[...])
    out_ref[...] = total


def shards(tokens, lengths, w_query, w_key, w_value, w_out, w_embed):
    section_idx = lax.axis_index("section")
    section_count = lax.axis_size("section")
    core_idx = lax.axis_index("tensor")
    group_count = lax.axis_size("dp")
    wq, wk, wv, wo = w_query[0], w_key[0], w_value[0], w_out[0]
    own = tokens[0]
    rows, half = own.shape
    pieces = 4
    width = half // pieces
    embed_half = w_embed.shape[1] // 2
    lens = lengths[:, 0]
    first_len = lax.dynamic_index_in_dim(lens, section_idx, 0, keepdims=False)
    last_len = lax.dynamic_index_in_dim(
        lens, (section_idx - (HOPS - 1)) % section_count, 0, keepdims=False
    )
    place = jnp.stack([core_idx.astype(jnp.int32), first_len, last_len])

    def shape(*dims, dtype=BF16):
        return jax.ShapeDtypeStruct(dims, dtype)

    with jax.named_scope("tokens_swap"):
        oth = exchanged(own, "tensor", 1)
    with jax.named_scope("weights_swap"):
        wo_oth = exchanged(wo, "tensor", 1)
        we_oth = exchanged(w_embed, "tensor", 1)
    with jax.named_scope("layer_one"):
        mixed = call(first_body, shape(rows, HD), 1, 5, 2 * rows * 2 * half * 3 * HD)(
            place, own, oth, wq, wk, wv
        )
        mixed_oth = exchanged(mixed, "tensor", 1)
        state = call(
            functools.partial(update_body, pieces),
            [shape(rows, width)] * pieces,
            1,
            5,
            2 * rows * 2 * HD * half,
        )(place, own, mixed, mixed_oth, wo, wo_oth)
    with jax.named_scope("hop"):
        state = [shifted(piece, "section", 1) for piece in state]
    with jax.named_scope("combine"):
        combined = call(
            combine_body, shape(2 * HD, embed_half), 1, 4, 2 * 2 * HD * 2 * half * embed_half
        )(place, wo, wo_oth, w_embed, we_oth)
    with jax.named_scope("layer_two"):
        state_oth = [exchanged(piece, "tensor", 1) for piece in state]
        mixed, embed_one = call(
            functools.partial(second_body, pieces),
            [shape(rows, HD), shape(rows, embed_half, dtype=F32)],
            1,
            2 * pieces + 5,
            2 * rows * 2 * half * (3 * HD + embed_half),
        )(place, *state, *state_oth, wq, wk, wv, w_embed, we_oth)
        mixed_oth = exchanged(mixed, "tensor", 1)
    with jax.named_scope("embed"):
        embed = call(embed_body, shape(rows, embed_half), 1, 4, 2 * rows * 2 * HD * embed_half)(
            place, embed_one, mixed, mixed_oth, combined
        )
        embeds = [embed] + [exchanged(embed, "dp", mask) for mask in range(1, group_count)]
    with jax.named_scope("moments"):
        gram = call(
            gram_body,
            shape(rows, rows * group_count, dtype=F32),
            0,
            group_count,
            2 * rows * rows * group_count * embed_half,
        )(*embeds)
        gram_oth = exchanged(gram, "tensor", 1)
        result = call(
            result_body,
            shape(rows, embed_half, dtype=F32),
            0,
            group_count + 2,
            2 * rows * rows * group_count * embed_half,
        )(*embeds, gram, gram_oth)
    return result[None]


def solution(mesh):
    return jax.shard_map(
        shards,
        mesh=mesh,
        in_specs=(
            P("section", "dp", "tensor"),
            P(None, "dp"),
            P("section", None, "tensor"),
            P("section", None, "tensor"),
            P("section", None, "tensor"),
            P("section", "tensor", None),
            P("tensor", None),
        ),
        out_specs=P("section", "dp", "tensor"),
        check_vma=False,
    )
```

```python
import functools
import math

import jax
import jax.numpy as jnp
from jax import lax
from jax.experimental import pallas as pl
from jax.experimental.pallas import tpu as pltpu
from jax.sharding import PartitionSpec as P

HD = 128
QKV = 3 * HD
EPSILON = 1e-05
BF16 = jnp.bfloat16
F32 = jnp.float32
VMEM_BYTES = 18 * 1024 * 1024
SHARES = (8, 8)


def shifted(value, axis, steps):
    count = lax.axis_size(axis)
    pairs = [(source, (source + steps) % count) for source in range(count)]
    return lax.ppermute(value, axis, pairs)


def exchanged(value, axis, mask):
    count = lax.axis_size(axis)
    return lax.ppermute(value, axis, [(source, source ^ mask) for source in range(count)])


def after(value, *others):
    return lax.optimization_barrier((value, *others))[0]


def dot(left, right):
    return lax.dot_general(left, right, (((1,), (0,)), ((), ())), preferred_element_type=F32)


def dot_t(left, right):
    return lax.dot_general(left, right, (((1,), (1,)), ((), ())), preferred_element_type=F32)


def shape(*dims, dtype=BF16):
    return jax.ShapeDtypeStruct(dims, dtype)


SPACES = {"s": pltpu.SMEM, "v": pltpu.VMEM, "h": pltpu.HBM}


def call(body, out_shapes, spaces, copies=0, last=False, scratch=()):
    kernel = pl.pallas_call(
        body,
        out_shape=out_shapes
        if last
        else jax.tree.map(lambda out: pltpu.VMEM(out.shape, out.dtype), out_shapes),
        in_specs=[pl.BlockSpec(memory_space=SPACES[space]) for space in spaces],
        out_specs=jax.tree.map(lambda _: pl.BlockSpec(memory_space=pltpu.VMEM), out_shapes),
        scratch_shapes=([pltpu.SemaphoreType.DMA((copies,))] if copies else []) + list(scratch),
        compiler_params=pltpu.CompilerParams(vmem_limit_bytes=VMEM_BYTES),
        cost_estimate=pl.CostEstimate(flops=0, bytes_accessed=0, transcendentals=0),
    )

    def place(operand, space):
        if space == "s":
            return operand
        return pltpu.with_memory_space_constraint(operand, SPACES[space])

    return lambda *operands: kernel(*map(place, operands, spaces))


def span(start, size):
    return pl.ds(pl.multiple_of(start, size), size)


def lane_sums(x):
    x32 = x.astype(F32)
    x2 = x32 * x32
    total = x2[:, :HD]
    for lane in range(HD, x.shape[1], HD):
        total += x2[:, lane : lane + HD]
    return total


def rms_scale(square, features):
    return lax.rsqrt(jnp.sum(square, axis=-1, keepdims=True) * (1.0 / features) + EPSILON)


def softmax_mix(qkv, live_len):
    query, key, value = (qkv[:, at : at + HD].astype(BF16) for at in range(0, QKV, HD))
    rows = query.shape[0]
    scores = dot_t(query, key) * (1.0 / math.sqrt(HD))
    key_pos = lax.broadcasted_iota(jnp.int32, (rows, rows), 1)
    scores = jnp.where(key_pos < live_len, scores, -1e30)
    weights = jnp.exp(scores - jnp.max(scores, axis=-1, keepdims=True))
    probs = (weights / jnp.sum(weights, axis=-1, keepdims=True)).astype(BF16)
    return dot(probs, value).astype(BF16)


def load_body(own_hbm, wq_hbm, wk_hbm, wv_hbm, own_ref, w_ref, qkv_ref, square_ref, sems):
    half = own_ref.shape[1]
    core = lax.axis_index("tensor")
    copies = [pltpu.make_async_copy(own_hbm.at[0], own_ref, sems.at[0])]
    for part in range(2):
        rows = span((core if part == 0 else 1 - core) * half, half)
        for at, w_hbm in enumerate((wq_hbm, wk_hbm, wv_hbm)):
            copies.append(
                pltpu.make_async_copy(
                    w_hbm.at[0, rows, :],
                    w_ref.at[rows, at * HD : (at + 1) * HD],
                    sems.at[len(copies)],
                )
            )
    for copy in copies:
        copy.start()
    copies[0].wait()
    own = own_ref[...]
    square_ref[...] = lane_sums(own)
    for copy in copies[1:4]:
        copy.wait()
    qkv_ref[...] = dot(own, w_ref[span(core * half, half), :])
    for copy in copies[4:]:
        copy.wait()


def first_body(
    lens_hbm, own_ref, oth_ref, w_ref, qkv_ref, square_ref, wo_hbm,
    held_ref, part_ref, wo_own_ref, wo_send_ref, sems, lens_ref,
):
    half = oth_ref.shape[1]
    core = lax.axis_index("tensor")
    copies = [
        pltpu.make_async_copy(wo_hbm.at[0, :, span(side * half, half)], ref, sems.at[index])
        for index, (side, ref) in enumerate(((1 - core, wo_send_ref), (core, wo_own_ref)))
    ]
    copies.append(pltpu.make_async_copy(lens_hbm, lens_ref, sems.at[2]))
    for copy in copies:
        copy.start()
    oth = oth_ref[...]
    qkv = qkv_ref[...] + dot(oth, w_ref[span((1 - core) * half, half), :])
    scale = rms_scale(square_ref[...] + lane_sums(oth), 2 * half)
    copies.pop().wait()
    mixed = softmax_mix(qkv * scale, lens_ref[lax.axis_index("section")])
    for copy in copies:
        copy.wait()
    part_ref[...] = dot(mixed, wo_send_ref[...]).astype(BF16)
    held_ref[...] = own_ref[...].astype(F32) + dot(mixed, wo_own_ref[...])


def update_body(held_ref, part_ref, *outs):
    lower = 0
    for out_ref in outs:
        upper = lower + out_ref.shape[1]
        held, part = held_ref[:, lower:upper], part_ref[:, lower:upper]
        out_ref[...] = (held + part.astype(F32)).astype(BF16)
        lower = upper


def combine_body(w_own_ref, w_oth_ref, e_hbm, e_ref, mine_ref, send_ref, sems):
    blocks = sems.shape[0]
    depth = e_ref.shape[0] // blocks
    copies = []
    for block in range(blocks):
        rows = slice(block * depth, (block + 1) * depth)
        copies.append(pltpu.make_async_copy(e_hbm.at[rows, :], e_ref.at[rows, :], sems.at[block]))
        copies[-1].start()
    cols = mine_ref.shape[1]
    core = lax.axis_index("tensor")
    weight = jnp.concatenate([w_own_ref[...], w_oth_ref[...]], axis=0)
    for copy in copies:
        copy.wait()
    mine_ref[...] = dot(weight, e_ref[:, span(core * cols, cols)])
    send_ref[...] = dot(weight, e_ref[:, span((1 - core) * cols, cols)])


def own_body(lower, own_ref, w_ref, e_ref, *refs):
    sums, (qkv_ref, square_ref, embed_ref) = refs[:-3], refs[-3:]
    width = own_ref.shape[1]
    half = e_ref.shape[0]
    src = pl.ds(pl.multiple_of(lax.axis_index("tensor") * half + lower, HD), width)
    x = own_ref[...]
    qkv, square, embed = dot(x, w_ref[src, :]), lane_sums(x), dot(x, e_ref[lower : lower + width, :])
    if sums:
        qkv, square = qkv + sums[0][...], square + sums[1][...]
        embed = embed + sums[2][...]
    qkv_ref[...], square_ref[...], embed_ref[...] = qkv, square, embed


def own_last_body(lower, own_ref, w_ref, e_ref, sum_ref, square_in_ref, embed_in_ref, *refs):
    qkv_ref, square_ref, mine_ref, send_ref = refs
    width = own_ref.shape[1]
    half = e_ref.shape[0]
    cols = mine_ref.shape[1]
    core = lax.axis_index("tensor")
    src = pl.ds(pl.multiple_of(core * half + lower, HD), width)
    x = own_ref[...]
    for side, out_ref in ((1 - core, send_ref), (core, mine_ref)):
        at = span(side * cols, cols)
        embed = embed_in_ref[:, at] + dot(x, e_ref[lower : lower + width, at])
        out_ref[...] = embed.astype(out_ref.dtype)
    qkv_ref[...] = sum_ref[...] + dot(x, w_ref[src, :])
    square_ref[...] = square_in_ref[...] + lane_sums(x)


def other_sums(lower, half, oth_ref, w_ref):
    src = pl.ds(
        pl.multiple_of((1 - lax.axis_index("tensor")) * half + lower, HD), oth_ref.shape[1]
    )
    x = oth_ref[...]
    return dot(x, w_ref[src, :]), lane_sums(x)


def other_body(lower, half, oth_ref, w_ref, sum_ref, square_in_ref, qkv_ref, square_ref):
    qkv, square = other_sums(lower, half, oth_ref, w_ref)
    qkv_ref[...] = sum_ref[...] + qkv
    square_ref[...] = square_in_ref[...] + square


def hop_anchor():
    sections = lax.axis_size("section")
    return lax.rem(lax.axis_index("section") + sections - 1, sections)


def second_body(lower, half, lens_ref, oth_ref, w_ref, sum_ref, square_in_ref, mixed_ref):
    qkv, square = other_sums(lower, half, oth_ref, w_ref)
    scale = rms_scale(square_in_ref[...] + square, 2 * half)
    mixed_ref[...] = softmax_mix((sum_ref[...] + qkv) * scale, lens_ref[hop_anchor()])


def combine_sum_body(mine_ref, recv_ref, out_ref):
    rows = mine_ref.shape[0] // 2
    out_ref[:rows, :] = (mine_ref[:rows, :] + recv_ref[rows:, :]).astype(BF16)
    out_ref[rows:, :] = (mine_ref[rows:, :] + recv_ref[:rows, :]).astype(BF16)


def embed_own_body(mine_ref, recv_ref, mixed_ref, combined_ref, out_ref):
    product = dot(mixed_ref[...], combined_ref[: mixed_ref.shape[1], :])
    out_ref[...] = mine_ref[...] + recv_ref[...].astype(F32) + product


def embed_body(lens_ref, sum_ref, mixed_ref, combined_ref, out_ref):
    embed = sum_ref[...] + dot(mixed_ref[...], combined_ref[mixed_ref.shape[1] :, :])
    row_pos = lax.broadcasted_iota(jnp.int32, embed.shape, 0)
    out_ref[...] = jnp.where(row_pos < lens_ref[hop_anchor()], embed, 0.0).astype(BF16)


def gram_body(*refs):
    own, embeds, out_ref = refs[0][...], refs[1:-1], refs[-1]
    rows = own.shape[0]
    for at, embed in enumerate(embeds):
        out_ref[:, at * rows : (at + 1) * rows] = dot_t(own, embed[...])


def result_body(tokens, first, *refs):
    (gram_own_ref, gram_oth_ref), embeds, out_ref = refs[:2], refs[2:-1], refs[-1]
    total = None
    if not first:
        embeds, total = embeds[:-1], embeds[-1][...]
    rows = embeds[0].shape[0]
    for at, embed in enumerate(embeds):
        cols = slice(at * rows, (at + 1) * rows)
        gram = (gram_own_ref[:, cols] + gram_oth_ref[:, cols]) * (1.0 / tokens)
        if first and at == 0:
            row = lax.broadcasted_iota(jnp.int32, gram.shape, 0)
            col = lax.broadcasted_iota(jnp.int32, gram.shape, 1)
            gram = gram - (row == col).astype(F32)
        product = dot(gram.astype(BF16), embed[...])
        total = product if total is None else total + product
    out_ref[...] = total


def shards(tokens, lengths, w_query, w_key, w_value, w_out, w_embed):
    group_count = lax.axis_size("dp")
    own_in = tokens[0]
    rows, half = own_in.shape
    features = 2 * half
    widths = [half * share // sum(SHARES) for share in SHARES]
    lowers = [sum(widths[:at]) for at in range(len(widths))]
    cols = w_embed.shape[1] // 2

    lens = lengths.reshape(-1)

    with jax.named_scope("layer_one"):
        oth = exchanged(own_in, "tensor", 1)
        own, w_own, qkv, square = call(
            load_body,
            [shape(rows, half), shape(features, QKV), shape(rows, QKV, dtype=F32), shape(rows, HD, dtype=F32)],
            "hhhh",
            7,
                    )(tokens, w_query, w_key, w_value)
        held, part, wo_own, wo_send = call(
            first_body,
            [shape(rows, half, dtype=F32)] + [shape(rows, half)] + [shape(HD, half)] * 2,
            "hvvvvvh",
            3,
            scratch=(pltpu.SMEM(lens.shape, jnp.int32),),
        )(lens, own, oth, w_own, qkv, square, w_out)
        part = exchanged(part, "tensor", 1)
        state = call(update_body, [shape(rows, width) for width in widths], "vv")(held, part)
    with jax.named_scope("weights"):
        wo_oth = exchanged(after(wo_send, state[0]), "tensor", 1)
    with jax.named_scope("hop"):
        state = [shifted(piece, "section", 1) for piece in state]
    with jax.named_scope("weights"):
        w_embed_own, c_mine, c_send = call(
            combine_body,
            [shape(*w_embed.shape)] + [shape(2 * HD, cols, dtype=F32)] * 2,
            "vvh",
            4,
        )(wo_own, wo_oth, after(w_embed, state[0]))
        combined = call(combine_sum_body, shape(2 * HD, cols), "vv")(
            c_mine, exchanged(c_send, "tensor", 1)
        )
    with jax.named_scope("layer_two"):
        sums = ()
        for lower, piece in zip(lowers, state):
            oth = exchanged(piece, "tensor", 1)
            if lower != lowers[-1]:
                qkv, square, embed = call(
                    functools.partial(own_body, lower),
                    [shape(rows, QKV, dtype=F32), shape(rows, HD, dtype=F32), shape(rows, 2 * cols, dtype=F32)],
                    "v" * (3 + len(sums)),
                )(piece, w_own, w_embed_own, *sums)
                qkv, square = call(
                    functools.partial(other_body, lower, half),
                    [shape(rows, QKV, dtype=F32), shape(rows, HD, dtype=F32)],
                    "vvvv",
                )(oth, w_own, qkv, square)
                sums = (qkv, square, embed)
            else:
                qkv, square, e_mine, e_send = call(
                    functools.partial(own_last_body, lower),
                    [shape(rows, QKV, dtype=F32), shape(rows, HD, dtype=F32)]
                    + [shape(rows, cols, dtype=F32), shape(rows, cols)],
                    "v" * 6,
                )(piece, w_own, w_embed_own, *sums)
        e_recv = exchanged(e_send, "tensor", 1)
        mixed = call(
            functools.partial(second_body, lower, half), shape(rows, HD), "svvvv"
        )(lens, oth, w_own, qkv, square)
        mixed_oth = exchanged(mixed, "tensor", 1)
        embed = call(embed_own_body, shape(rows, cols, dtype=F32), "vvvv")(
            e_mine, e_recv, mixed, combined
        )
        embed = call(embed_body, shape(rows, cols), "svvv")(lens, embed, mixed_oth, combined)
    with jax.named_scope("moments"):
        embeds = [embed] + [exchanged(embed, "dp", mask) for mask in range(1, group_count)]
        result = ()
        for part in (embeds[:2], embeds[2:]):
            gram = call(gram_body, shape(rows, rows * len(part), dtype=F32), "v" * (1 + len(part)))(
                embed, *part
            )
            operands = (gram, exchanged(gram, "tensor", 1), *part, *result)
            result = (
                call(
                    functools.partial(result_body, rows * group_count, not result),
                    shape(rows, cols, dtype=F32),
                    "v" * len(operands),
                    last=bool(result),
                )(*operands),
            )
    return result[0][None]


def solution(mesh):
    return jax.shard_map(
        shards,
        mesh=mesh,
        in_specs=(
            P("section", "dp", "tensor"),
            P(None, "dp"),
            P("section", None, "tensor"),
            P("section", None, "tensor"),
            P("section", None, "tensor"),
            P("section", "tensor", None),
            P("tensor", None),
        ),
        out_specs=P("section", "dp", "tensor"),
        check_vma=False,
    )
```

```python
import functools
import math

import jax
import jax.numpy as jnp
from jax import lax
from jax.experimental import pallas as pl
from jax.experimental.pallas import tpu as pltpu
from jax.sharding import PartitionSpec as P

HD = 128
QKV = 3 * HD
EPSILON = 1e-05
BF16 = jnp.bfloat16
F32 = jnp.float32
VMEM_BYTES = 18 * 1024 * 1024
SHARES = (7, 9)
DP_ORDER = lambda count: reversed(range(1, count))


def shifted(value, axis, steps):
    count = lax.axis_size(axis)
    pairs = [(source, (source + steps) % count) for source in range(count)]
    return lax.ppermute(value, axis, pairs)


def exchanged(value, axis, mask):
    count = lax.axis_size(axis)
    return lax.ppermute(value, axis, [(source, source ^ mask) for source in range(count)])


def after(value, *others):
    return lax.optimization_barrier((value, *others))[0]


def dot(left, right):
    return lax.dot_general(left, right, (((1,), (0,)), ((), ())), preferred_element_type=F32)


def dot_t(left, right):
    return lax.dot_general(left, right, (((1,), (1,)), ((), ())), preferred_element_type=F32)


def shape(*dims, dtype=BF16):
    return jax.ShapeDtypeStruct(dims, dtype)


SPACES = {"s": pltpu.SMEM, "v": pltpu.VMEM, "h": pltpu.HBM}


def call(body, out_shapes, spaces, copies=0, last=False, scratch=()):
    kernel = pl.pallas_call(
        body,
        out_shape=out_shapes
        if last
        else jax.tree.map(lambda out: pltpu.VMEM(out.shape, out.dtype), out_shapes),
        in_specs=[pl.BlockSpec(memory_space=SPACES[space]) for space in spaces],
        out_specs=jax.tree.map(lambda _: pl.BlockSpec(memory_space=pltpu.VMEM), out_shapes),
        scratch_shapes=([pltpu.SemaphoreType.DMA((copies,))] if copies else []) + list(scratch),
        compiler_params=pltpu.CompilerParams(vmem_limit_bytes=VMEM_BYTES),
        cost_estimate=pl.CostEstimate(flops=0, bytes_accessed=0, transcendentals=0),
    )

    def place(operand, space):
        if space == "s":
            return operand
        return pltpu.with_memory_space_constraint(operand, SPACES[space])

    return lambda *operands: kernel(*map(place, operands, spaces))


def span(start, size):
    return pl.ds(pl.multiple_of(start, size), size)


def lane_sums(x):
    x32 = x.astype(F32)
    x2 = x32 * x32
    total = x2[:, :HD]
    for lane in range(HD, x.shape[1], HD):
        total += x2[:, lane : lane + HD]
    return total


def rms_scale(square, features):
    return lax.rsqrt(jnp.sum(square, axis=-1, keepdims=True) * (1.0 / features) + EPSILON)


def softmax_mix(qkv, live_len):
    query, key, value = (qkv[:, at : at + HD].astype(BF16) for at in range(0, QKV, HD))
    rows = query.shape[0]
    scores = dot_t(query, key) * (1.0 / math.sqrt(HD))
    key_pos = lax.broadcasted_iota(jnp.int32, (rows, rows), 1)
    scores = jnp.where(key_pos < live_len, scores, -1e30)
    weights = jnp.exp(scores - jnp.max(scores, axis=-1, keepdims=True))
    probs = (weights / jnp.sum(weights, axis=-1, keepdims=True)).astype(BF16)
    return dot(probs, value).astype(BF16)


def load_body(own_hbm, wq_hbm, wk_hbm, wv_hbm, own_ref, w_ref, qkv_ref, square_ref, sems):
    half = own_ref.shape[1]
    core = lax.axis_index("tensor")
    copies = [pltpu.make_async_copy(own_hbm.at[0], own_ref, sems.at[0])]
    for part in range(2):
        rows = span((core if part == 0 else 1 - core) * half, half)
        for at, w_hbm in enumerate((wq_hbm, wk_hbm, wv_hbm)):
            copies.append(
                pltpu.make_async_copy(
                    w_hbm.at[0, rows, :],
                    w_ref.at[rows, at * HD : (at + 1) * HD],
                    sems.at[len(copies)],
                )
            )
    for copy in copies:
        copy.start()
    copies[0].wait()
    own = own_ref[...]
    square_ref[...] = lane_sums(own)
    for copy in copies[1:4]:
        copy.wait()
    qkv_ref[...] = dot(own, w_ref[span(core * half, half), :])
    for copy in copies[4:]:
        copy.wait()


def first_body(
    lens_hbm, oth_ref, w_ref, qkv_ref, square_ref, wo_hbm,
    mixed_ref, part_ref, wo_own_ref, wo_send_ref, sems, lens_ref,
):
    half = oth_ref.shape[1]
    core = lax.axis_index("tensor")
    copies = [
        pltpu.make_async_copy(wo_hbm.at[0, :, span(side * half, half)], ref, sems.at[index])
        for index, (side, ref) in enumerate(((1 - core, wo_send_ref), (core, wo_own_ref)))
    ]
    copies.append(pltpu.make_async_copy(lens_hbm, lens_ref, sems.at[2]))
    for copy in copies:
        copy.start()
    oth = oth_ref[...]
    qkv = qkv_ref[...] + dot(oth, w_ref[span((1 - core) * half, half), :])
    scale = rms_scale(square_ref[...] + lane_sums(oth), 2 * half)
    copies.pop().wait()
    mixed = softmax_mix(qkv * scale, lens_ref[lax.axis_index("section")])
    copies[0].wait()
    part_ref[...] = dot(mixed, wo_send_ref[...]).astype(BF16)
    mixed_ref[...] = mixed
    copies[1].wait()


def held_body(own_ref, mixed_ref, wo_own_ref, held_ref):
    held_ref[...] = own_ref[...].astype(F32) + dot(mixed_ref[...], wo_own_ref[...])


def update_body(held_ref, part_ref, *outs):
    lower = 0
    for out_ref in outs:
        upper = lower + out_ref.shape[1]
        held, part = held_ref[:, lower:upper], part_ref[:, lower:upper]
        out_ref[...] = (held + part.astype(F32)).astype(BF16)
        lower = upper


def combine_body(lens_ref, w_own_ref, w_oth_ref, e_hbm, e_ref, mine_ref, send_ref, live_ref, sems):
    blocks = sems.shape[0]
    depth = e_ref.shape[0] // blocks
    copies = []
    for block in range(blocks):
        rows = slice(block * depth, (block + 1) * depth)
        copies.append(pltpu.make_async_copy(e_hbm.at[rows, :], e_ref.at[rows, :], sems.at[block]))
        copies[-1].start()
    cols = mine_ref.shape[1]
    core = lax.axis_index("tensor")
    weight = jnp.concatenate([w_own_ref[...], w_oth_ref[...]], axis=0)
    live_ref[...] = jnp.full(live_ref.shape, lens_ref[hop_anchor()], jnp.int32)
    for copy in copies:
        copy.wait()
    mine_ref[...] = dot(weight, e_ref[:, span(core * cols, cols)])
    send_ref[...] = dot(weight, e_ref[:, span((1 - core) * cols, cols)]).astype(BF16)


def own_body(lower, own_ref, w_ref, e_ref, *refs):
    sums, (qkv_ref, square_ref, embed_ref) = refs[:-3], refs[-3:]
    width = own_ref.shape[1]
    half = e_ref.shape[0]
    src = pl.ds(pl.multiple_of(lax.axis_index("tensor") * half + lower, HD), width)
    x = own_ref[...]
    qkv, square, embed = dot(x, w_ref[src, :]), lane_sums(x), dot(x, e_ref[lower : lower + width, :])
    if sums:
        qkv, square = qkv + sums[0][...], square + sums[1][...]
        embed = embed + sums[2][...]
    qkv_ref[...], square_ref[...], embed_ref[...] = qkv, square, embed


def own_last_body(lower, own_ref, w_ref, e_ref, sum_ref, square_in_ref, embed_in_ref, *refs):
    qkv_ref, square_ref, mine_ref, send_ref = refs
    width = own_ref.shape[1]
    half = e_ref.shape[0]
    cols = mine_ref.shape[1]
    core = lax.axis_index("tensor")
    src = pl.ds(pl.multiple_of(core * half + lower, HD), width)
    x = own_ref[...]
    for side, out_ref in ((1 - core, send_ref), (core, mine_ref)):
        at = span(side * cols, cols)
        embed = embed_in_ref[:, at] + dot(x, e_ref[lower : lower + width, at])
        out_ref[...] = embed.astype(out_ref.dtype)
    qkv_ref[...] = sum_ref[...] + dot(x, w_ref[src, :])
    square_ref[...] = square_in_ref[...] + lane_sums(x)


def other_sums(lower, half, oth_ref, w_ref):
    src = pl.ds(
        pl.multiple_of((1 - lax.axis_index("tensor")) * half + lower, HD), oth_ref.shape[1]
    )
    x = oth_ref[...]
    return dot(x, w_ref[src, :]), lane_sums(x)


def other_body(lower, half, oth_ref, w_ref, sum_ref, square_in_ref, qkv_ref, square_ref):
    qkv, square = other_sums(lower, half, oth_ref, w_ref)
    qkv_ref[...] = sum_ref[...] + qkv
    square_ref[...] = square_in_ref[...] + square


def hop_anchor():
    sections = lax.axis_size("section")
    return lax.rem(lax.axis_index("section") + sections - 1, sections)


def second_body(lower, half, live_ref, oth_ref, w_ref, sum_ref, square_in_ref, mixed_ref):
    qkv, square = other_sums(lower, half, oth_ref, w_ref)
    scale = rms_scale(square_in_ref[...] + square, 2 * half)
    mixed_ref[...] = softmax_mix((sum_ref[...] + qkv) * scale, live_ref[...])


def combine_sum_body(mine_ref, recv_ref, out_ref):
    rows = mine_ref.shape[0] // 2
    out_ref[:rows, :] = (mine_ref[:rows, :] + recv_ref[rows:, :]).astype(BF16)
    out_ref[rows:, :] = (mine_ref[rows:, :] + recv_ref[:rows, :]).astype(BF16)


def embed_own_body(mine_ref, recv_ref, mixed_ref, combined_ref, out_ref):
    product = dot(mixed_ref[...], combined_ref[: mixed_ref.shape[1], :])
    out_ref[...] = mine_ref[...] + recv_ref[...].astype(F32) + product


def embed_body(live_ref, sum_ref, mixed_ref, combined_ref, out_ref):
    embed = sum_ref[...] + dot(mixed_ref[...], combined_ref[mixed_ref.shape[1] :, :])
    live = live_ref[...]
    keep = lax.broadcasted_iota(jnp.int32, live.shape, 0) < live
    for lane in range(0, embed.shape[1], HD):
        cols = slice(lane, lane + HD)
        out_ref[:, cols] = jnp.where(keep, embed[:, cols], 0.0).astype(BF16)


def gram_body(*refs):
    own, embeds, out_ref = refs[0][...], refs[1:-1], refs[-1]
    rows = own.shape[0]
    for at, embed in enumerate(embeds):
        out_ref[:, at * rows : (at + 1) * rows] = dot_t(own, embed[...])


def result_body(tokens, first, *refs):
    (gram_own_ref, gram_oth_ref), embeds, out_ref = refs[:2], refs[2:-1], refs[-1]
    total = None
    if not first:
        embeds, total = embeds[:-1], embeds[-1][...]
    rows = embeds[0].shape[0]
    for at, embed in enumerate(embeds):
        cols = slice(at * rows, (at + 1) * rows)
        gram = (gram_own_ref[:, cols] + gram_oth_ref[:, cols]) * (1.0 / tokens)
        if first and at == 0:
            row = lax.broadcasted_iota(jnp.int32, gram.shape, 0)
            col = lax.broadcasted_iota(jnp.int32, gram.shape, 1)
            gram = gram - (row == col).astype(F32)
        product = dot(gram.astype(BF16), embed[...])
        total = product if total is None else total + product
    out_ref[...] = total


def shards(tokens, lengths, w_query, w_key, w_value, w_out, w_embed):
    group_count = lax.axis_size("dp")
    own_in = tokens[0]
    rows, half = own_in.shape
    features = 2 * half
    widths = [half * share // sum(SHARES) for share in SHARES]
    lowers = [sum(widths[:at]) for at in range(len(widths))]
    cols = w_embed.shape[1] // 2

    lens = lengths.reshape(-1)

    with jax.named_scope("layer_one"):
        oth = exchanged(own_in, "tensor", 1)
        own, w_own, qkv, square = call(
            load_body,
            [shape(rows, half), shape(features, QKV), shape(rows, QKV, dtype=F32), shape(rows, HD, dtype=F32)],
            "hhhh",
            7,
                    )(tokens, w_query, w_key, w_value)
        mixed, part, wo_own, wo_send = call(
            first_body,
            [shape(rows, HD), shape(rows, half)] + [shape(HD, half)] * 2,
            "hvvvvh",
            3,
            scratch=(pltpu.SMEM(lens.shape, jnp.int32),),
        )(lens, oth, w_own, qkv, square, w_out)
        part = exchanged(part, "tensor", 1)
        held = call(held_body, shape(rows, half, dtype=F32), "vvv")(own, mixed, wo_own)
        state = call(update_body, [shape(rows, width) for width in widths], "vv")(held, part)
    with jax.named_scope("weights"):
        wo_oth = exchanged(after(wo_send, state[0]), "tensor", 1)
    with jax.named_scope("hop"):
        state = [shifted(piece, "section", 1) for piece in state]
    with jax.named_scope("weights"):
        w_embed_own, c_mine, c_send, live = call(
            combine_body,
            [shape(*w_embed.shape)]
            + [shape(2 * HD, cols, dtype=F32), shape(2 * HD, cols)]
            + [shape(rows, HD, dtype=jnp.int32)],
            "svvh",
            4,
        )(lens, wo_own, wo_oth, w_embed)
        combined = call(combine_sum_body, shape(2 * HD, cols), "vv")(
            c_mine, exchanged(c_send, "tensor", 1)
        )
    with jax.named_scope("layer_two"):
        sums = ()
        for lower, piece in zip(lowers, state):
            if sums:
                piece, combined, *sums = lax.optimization_barrier((piece, combined, *sums))
            oth = exchanged(piece, "tensor", 1)
            if lower != lowers[-1]:
                qkv, square, embed = call(
                    functools.partial(own_body, lower),
                    [shape(rows, QKV, dtype=F32), shape(rows, HD, dtype=F32), shape(rows, 2 * cols, dtype=F32)],
                    "v" * (3 + len(sums)),
                )(piece, w_own, w_embed_own, *sums)
                qkv, square = call(
                    functools.partial(other_body, lower, half),
                    [shape(rows, QKV, dtype=F32), shape(rows, HD, dtype=F32)],
                    "vvvv",
                )(oth, w_own, qkv, square)
                sums = (qkv, square, embed)
            else:
                qkv, square, e_mine, e_send = call(
                    functools.partial(own_last_body, lower),
                    [shape(rows, QKV, dtype=F32), shape(rows, HD, dtype=F32)]
                    + [shape(rows, cols, dtype=F32), shape(rows, cols)],
                    "v" * 6,
                )(piece, w_own, w_embed_own, *sums)
        e_recv = exchanged(e_send, "tensor", 1)
        mixed = call(
            functools.partial(second_body, lower, half), shape(rows, HD), "vvvvv"
        )(live, oth, w_own, qkv, square)
        mixed_oth = exchanged(mixed, "tensor", 1)
        embed = call(embed_own_body, shape(rows, cols, dtype=F32), "vvvv")(
            e_mine, e_recv, mixed, combined
        )
        embed = call(embed_body, shape(rows, cols), "vvvv")(live, embed, mixed_oth, combined)
    with jax.named_scope("moments"):
        embeds = [embed] + [exchanged(embed, "dp", mask) for mask in DP_ORDER(group_count)]
        result = ()
        for part in (embeds[:2], embeds[2:]):
            gram = call(gram_body, shape(rows, rows * len(part), dtype=F32), "v" * (1 + len(part)))(
                embed, *part
            )
            operands = (gram, exchanged(gram, "tensor", 1), *part, *result)
            result = (
                call(
                    functools.partial(result_body, rows * group_count, not result),
                    shape(rows, cols, dtype=F32),
                    "v" * len(operands),
                    last=bool(result),
                )(*operands),
            )
    return result[0][None]


def solution(mesh):
    return jax.shard_map(
        shards,
        mesh=mesh,
        in_specs=(
            P("section", "dp", "tensor"),
            P(None, "dp"),
            P("section", None, "tensor"),
            P("section", None, "tensor"),
            P("section", None, "tensor"),
            P("section", "tensor", None),
            P("tensor", None),
        ),
        out_specs=P("section", "dp", "tensor"),
        check_vma=False,
    )
```

```python
import functools
import math

import jax
import jax.numpy as jnp
from jax import lax
from jax.experimental import pallas as pl
from jax.experimental.pallas import tpu as pltpu
from jax.sharding import PartitionSpec as P

HD = 128
QKV = 3 * HD
EPSILON = 1e-05
BF16 = jnp.bfloat16
F32 = jnp.float32
VMEM_BYTES = 18 * 1024 * 1024
SHARES = (7, 9)
WO_PARTS = 4
DP_ORDER = lambda count: reversed(range(1, count))


def shifted(value, axis, steps):
    count = lax.axis_size(axis)
    pairs = [(source, (source + steps) % count) for source in range(count)]
    return lax.ppermute(value, axis, pairs)


def exchanged(value, axis, mask):
    count = lax.axis_size(axis)
    return lax.ppermute(value, axis, [(source, source ^ mask) for source in range(count)])


def after(value, *others):
    return lax.optimization_barrier((value, *others))[0]


def dot(left, right):
    return lax.dot_general(left, right, (((1,), (0,)), ((), ())), preferred_element_type=F32)


def dot_t(left, right):
    return lax.dot_general(left, right, (((1,), (1,)), ((), ())), preferred_element_type=F32)


def shape(*dims, dtype=BF16):
    return jax.ShapeDtypeStruct(dims, dtype)


SPACES = {"s": pltpu.SMEM, "v": pltpu.VMEM, "h": pltpu.HBM}


def call(body, out_shapes, spaces, copies=0, last=False, scratch=()):
    kernel = pl.pallas_call(
        body,
        out_shape=out_shapes
        if last
        else jax.tree.map(lambda out: pltpu.VMEM(out.shape, out.dtype), out_shapes),
        in_specs=[pl.BlockSpec(memory_space=SPACES[space]) for space in spaces],
        out_specs=jax.tree.map(
            lambda _: pl.BlockSpec(memory_space=pltpu.HBM if last else pltpu.VMEM), out_shapes
        ),
        scratch_shapes=([pltpu.SemaphoreType.DMA((copies,))] if copies else []) + list(scratch),
        compiler_params=pltpu.CompilerParams(vmem_limit_bytes=VMEM_BYTES),
        cost_estimate=pl.CostEstimate(flops=0, bytes_accessed=0, transcendentals=0),
    )

    def place(operand, space):
        if space == "s":
            return operand
        return pltpu.with_memory_space_constraint(operand, SPACES[space])

    return lambda *operands: kernel(*map(place, operands, spaces))


def span(start, size):
    return pl.ds(pl.multiple_of(start, size), size)


def lane_sums(x):
    x32 = x.astype(F32)
    x2 = x32 * x32
    total = x2[:, :HD]
    for lane in range(HD, x.shape[1], HD):
        total += x2[:, lane : lane + HD]
    return total


def rms_scale(square, features):
    return lax.rsqrt(jnp.sum(square, axis=-1, keepdims=True) * (1.0 / features) + EPSILON)


def softmax_mix(qkv, live_len):
    query, key, value = (qkv[:, at : at + HD].astype(BF16) for at in range(0, QKV, HD))
    rows = query.shape[0]
    scores = dot_t(query, key) * (1.0 / math.sqrt(HD))
    key_pos = lax.broadcasted_iota(jnp.int32, (rows, rows), 1)
    scores = jnp.where(key_pos < live_len, scores, -1e30)
    weights = jnp.exp(scores - jnp.max(scores, axis=-1, keepdims=True))
    probs = (weights / jnp.sum(weights, axis=-1, keepdims=True)).astype(BF16)
    return dot(probs, value).astype(BF16)


def load_body(
    lens_hbm, own_hbm, wq_hbm, wk_hbm, wv_hbm, wo_hbm,
    own_ref, w_ref, qkv_ref, square_ref, live_ref, *rest,
):
    wo_own_ref, *wo_send_refs, sems, lens_ref = rest
    half = own_ref.shape[1]
    core = lax.axis_index("tensor")
    pairs = [(lens_hbm, lens_ref), (own_hbm.at[0], own_ref)]
    for side in (core, 1 - core):
        rows = span(side * half, half)
        for at, w_hbm in enumerate((wq_hbm, wk_hbm, wv_hbm)):
            pairs.append((w_hbm.at[0, rows, :], w_ref.at[rows, at * HD : (at + 1) * HD]))
    for at, ref in enumerate(wo_send_refs):
        width = ref.shape[1]
        pairs.append((wo_hbm.at[0, :, span((1 - core) * half + at * width, width)], ref))
    pairs.append((wo_hbm.at[0, :, span(core * half, half)], wo_own_ref))
    copies = [
        pltpu.make_async_copy(source, target, sems.at[index])
        for index, (source, target) in enumerate(pairs)
    ]
    for copy in copies:
        copy.start()
    copies[0].wait()
    live_ref[...] = jnp.full(live_ref.shape, lens_ref[lax.axis_index("section")], jnp.int32)
    copies[1].wait()
    own = own_ref[...]
    square_ref[...] = lane_sums(own)
    for copy in copies[2:5]:
        copy.wait()
    qkv_ref[...] = dot(own, w_ref[span(core * half, half), :])
    for copy in copies[5:]:
        copy.wait()


def first_body(live_ref, oth_ref, w_ref, qkv_ref, square_ref, *refs):
    wo_send_refs, mixed_ref, parts = refs[:WO_PARTS], refs[WO_PARTS], refs[WO_PARTS + 1 :]
    half = oth_ref.shape[1]
    core = lax.axis_index("tensor")
    oth = oth_ref[...]
    qkv = qkv_ref[...] + dot(oth, w_ref[span((1 - core) * half, half), :])
    scale = rms_scale(square_ref[...] + lane_sums(oth), 2 * half)
    mixed = softmax_mix(qkv * scale, live_ref[...])
    mixed_ref[...] = mixed
    weight = jnp.concatenate([ref[...] for ref in wo_send_refs], axis=1)
    lower = 0
    for part_ref in parts:
        upper = lower + part_ref.shape[1]
        part_ref[...] = dot(mixed, weight[:, lower:upper]).astype(BF16)
        lower = upper


def held_body(own_ref, mixed_ref, wo_own_ref, held_ref):
    held_ref[...] = own_ref[...].astype(F32) + dot(mixed_ref[...], wo_own_ref[...])


def update_body(lower, held_ref, *refs):
    parts, out_ref = refs[:-1], refs[-1]
    width = out_ref.shape[1]
    part = jnp.concatenate([ref[...] for ref in parts], axis=1)
    part = part[:, part.shape[1] - width :] if len(parts) > 1 else part[:, :width]
    held = held_ref[:, lower : lower + width]
    out_ref[...] = (held + part.astype(F32)).astype(BF16)


def combine_body(lens_ref, w_own_ref, e_hbm, *refs):
    w_oth_refs, (e_ref, mine_ref, send_ref, live_ref, sems) = refs[:WO_PARTS], refs[WO_PARTS:]
    blocks = sems.shape[0]
    depth = e_ref.shape[0] // blocks
    copies = []
    for block in range(blocks):
        rows = slice(block * depth, (block + 1) * depth)
        copies.append(pltpu.make_async_copy(e_hbm.at[rows, :], e_ref.at[rows, :], sems.at[block]))
        copies[-1].start()
    cols = mine_ref.shape[1]
    core = lax.axis_index("tensor")
    w_oth = jnp.concatenate([ref[...] for ref in w_oth_refs], axis=1)
    weight = jnp.concatenate([w_own_ref[...], w_oth], axis=0)
    live_ref[...] = jnp.full(live_ref.shape, lens_ref[hop_anchor()], jnp.int32)
    for copy in copies:
        copy.wait()
    mine_ref[...] = dot(weight, e_ref[:, span(core * cols, cols)])
    send_ref[...] = dot(weight, e_ref[:, span((1 - core) * cols, cols)]).astype(BF16)


def own_body(lower, own_ref, w_ref, e_ref, *refs):
    sums, (qkv_ref, square_ref, embed_ref) = refs[:-3], refs[-3:]
    width = own_ref.shape[1]
    half = e_ref.shape[0]
    src = pl.ds(pl.multiple_of(lax.axis_index("tensor") * half + lower, HD), width)
    x = own_ref[...]
    qkv, square, embed = dot(x, w_ref[src, :]), lane_sums(x), dot(x, e_ref[lower : lower + width, :])
    if sums:
        qkv, square = qkv + sums[0][...], square + sums[1][...]
        embed = embed + sums[2][...]
    qkv_ref[...], square_ref[...], embed_ref[...] = qkv, square, embed


def own_last_body(lower, own_ref, w_ref, e_ref, sum_ref, square_in_ref, embed_in_ref, *refs):
    qkv_ref, square_ref, mine_ref, send_ref = refs
    width = own_ref.shape[1]
    half = e_ref.shape[0]
    cols = mine_ref.shape[1]
    core = lax.axis_index("tensor")
    src = pl.ds(pl.multiple_of(core * half + lower, HD), width)
    x = own_ref[...]
    for side, out_ref in ((1 - core, send_ref), (core, mine_ref)):
        at = span(side * cols, cols)
        embed = embed_in_ref[:, at] + dot(x, e_ref[lower : lower + width, at])
        out_ref[...] = embed.astype(out_ref.dtype)
    qkv_ref[...] = sum_ref[...] + dot(x, w_ref[src, :])
    square_ref[...] = square_in_ref[...] + lane_sums(x)


def other_sums(lower, half, oth_ref, w_ref):
    src = pl.ds(
        pl.multiple_of((1 - lax.axis_index("tensor")) * half + lower, HD), oth_ref.shape[1]
    )
    x = oth_ref[...]
    return dot(x, w_ref[src, :]), lane_sums(x)


def other_body(lower, half, oth_ref, w_ref, sum_ref, square_in_ref, qkv_ref, square_ref):
    qkv, square = other_sums(lower, half, oth_ref, w_ref)
    qkv_ref[...] = sum_ref[...] + qkv
    square_ref[...] = square_in_ref[...] + square


def hop_anchor():
    sections = lax.axis_size("section")
    return lax.rem(lax.axis_index("section") + sections - 1, sections)


def second_body(lower, half, live_ref, oth_ref, w_ref, sum_ref, square_in_ref, mixed_ref):
    qkv, square = other_sums(lower, half, oth_ref, w_ref)
    scale = rms_scale(square_in_ref[...] + square, 2 * half)
    mixed_ref[...] = softmax_mix((sum_ref[...] + qkv) * scale, live_ref[...])


def combine_sum_body(mine_ref, recv_ref, out_ref):
    rows = mine_ref.shape[0] // 2
    out_ref[:rows, :] = (mine_ref[:rows, :] + recv_ref[rows:, :]).astype(BF16)
    out_ref[rows:, :] = (mine_ref[rows:, :] + recv_ref[:rows, :]).astype(BF16)


def embed_own_body(mine_ref, recv_ref, mixed_ref, combined_ref, out_ref):
    product = dot(mixed_ref[...], combined_ref[: mixed_ref.shape[1], :])
    out_ref[...] = mine_ref[...] + recv_ref[...].astype(F32) + product


def embed_body(live_ref, sum_ref, mixed_ref, combined_ref, out_ref):
    embed = sum_ref[...] + dot(mixed_ref[...], combined_ref[mixed_ref.shape[1] :, :])
    live = live_ref[...]
    keep = lax.broadcasted_iota(jnp.int32, live.shape, 0) < live
    for lane in range(0, embed.shape[1], HD):
        cols = slice(lane, lane + HD)
        out_ref[:, cols] = jnp.where(keep, embed[:, cols], 0.0).astype(BF16)


def gram_body(*refs):
    own, embeds, out_ref = refs[0][...], refs[1:-1], refs[-1]
    rows = own.shape[0]
    for at, embed in enumerate(embeds):
        out_ref[:, at * rows : (at + 1) * rows] = dot_t(own, embed[...])


def result_sums(tokens, first, gram_own_ref, gram_oth_ref, embeds):
    rows = embeds[0].shape[0]
    gram = (gram_own_ref[...] + gram_oth_ref[...]) * (1.0 / tokens)
    if first:
        row = lax.broadcasted_iota(jnp.int32, gram.shape, 0)
        col = lax.broadcasted_iota(jnp.int32, gram.shape, 1)
        gram = gram - (row == col).astype(F32)
    gram = gram.astype(BF16)
    return lambda cols: dot(
        gram, jnp.concatenate([embed[:, cols] for embed in embeds], axis=0)
    )


def result_body(tokens, gram_own_ref, gram_oth_ref, *refs):
    embeds, out_ref = refs[:-1], refs[-1]
    out_ref[...] = result_sums(tokens, True, gram_own_ref, gram_oth_ref, embeds)(slice(None))


def result_last_body(tokens, gram_own_ref, gram_oth_ref, *refs):
    embeds, (sum_ref, out_hbm, sems, out_ref) = refs[:-4], refs[-4:]
    product = result_sums(tokens, False, gram_own_ref, gram_oth_ref, embeds)
    chunks = sems.shape[0]
    width = out_ref.shape[1] // chunks
    copies = []
    for chunk in range(chunks):
        cols = slice(chunk * width, (chunk + 1) * width)
        out_ref[:, cols] = sum_ref[:, cols] + product(cols)
        copies.append(
            pltpu.make_async_copy(out_ref.at[:, cols], out_hbm.at[:, cols], sems.at[chunk])
        )
        copies[-1].start()
    for copy in copies:
        copy.wait()


def shards(tokens, lengths, w_query, w_key, w_value, w_out, w_embed):
    group_count = lax.axis_size("dp")
    own_in = tokens[0]
    rows, half = own_in.shape
    features = 2 * half
    widths = [half * share // sum(SHARES) for share in SHARES]
    lowers = [sum(widths[:at]) for at in range(len(widths))]
    cols = w_embed.shape[1] // 2

    lens = lengths.reshape(-1)

    with jax.named_scope("layer_one"):
        oth = exchanged(own_in, "tensor", 1)
        own, w_own, qkv, square, live, wo_own, *wo_send = call(
            load_body,
            [
                shape(rows, half),
                shape(features, QKV),
                shape(rows, QKV, dtype=F32),
                shape(rows, HD, dtype=F32),
                shape(rows, HD, dtype=jnp.int32),
                shape(HD, half),
            ]
            + [shape(HD, half // WO_PARTS)] * WO_PARTS,
            "hhhhhh",
            9 + WO_PARTS,
            scratch=(pltpu.SMEM(lens.shape, jnp.int32),),
        )(lens, tokens, w_query, w_key, w_value, w_out)
        mixed, *parts = call(
            first_body, [shape(rows, HD)] + [shape(rows, half // 2)] * 2, "v" * (5 + WO_PARTS)
        )(live, oth, w_own, qkv, square, *wo_send)
        parts = [exchanged(part, "tensor", 1) for part in parts]
        held = call(held_body, shape(rows, half, dtype=F32), "vvv")(own, mixed, wo_own)
        state = []
        for lower, width in zip(lowers, widths):
            needed = parts if lower else parts[:1]
            body = functools.partial(update_body, lower)
            state.append(call(body, shape(rows, width), "v" * (1 + len(needed)))(held, *needed))
    with jax.named_scope("weights"):
        wo_oth = [exchanged(after(part, state[-1]), "tensor", 1) for part in wo_send]
    with jax.named_scope("hop"):
        state = [shifted(piece, "section", 1) for piece in state]
    with jax.named_scope("weights"):
        w_embed_own, c_mine, c_send, live = call(
            combine_body,
            [shape(*w_embed.shape)]
            + [shape(2 * HD, cols, dtype=F32), shape(2 * HD, cols)]
            + [shape(rows, HD, dtype=jnp.int32)],
            "svh" + "v" * WO_PARTS,
            4,
        )(lens, wo_own, w_embed, *wo_oth)
        combined = call(combine_sum_body, shape(2 * HD, cols), "vv")(
            c_mine, exchanged(c_send, "tensor", 1)
        )
    with jax.named_scope("layer_two"):
        sums = ()
        for lower, piece in zip(lowers, state):
            if sums:
                piece, combined, *sums = lax.optimization_barrier((piece, combined, *sums))
            oth = exchanged(piece, "tensor", 1)
            if lower != lowers[-1]:
                qkv, square, embed = call(
                    functools.partial(own_body, lower),
                    [shape(rows, QKV, dtype=F32), shape(rows, HD, dtype=F32), shape(rows, 2 * cols, dtype=F32)],
                    "v" * (3 + len(sums)),
                )(piece, w_own, w_embed_own, *sums)
                qkv, square = call(
                    functools.partial(other_body, lower, half),
                    [shape(rows, QKV, dtype=F32), shape(rows, HD, dtype=F32)],
                    "vvvv",
                )(oth, w_own, qkv, square)
                sums = (qkv, square, embed)
            else:
                qkv, square, e_mine, e_send = call(
                    functools.partial(own_last_body, lower),
                    [shape(rows, QKV, dtype=F32), shape(rows, HD, dtype=F32)]
                    + [shape(rows, cols, dtype=F32), shape(rows, cols)],
                    "v" * 6,
                )(piece, w_own, w_embed_own, *sums)
        e_recv = exchanged(e_send, "tensor", 1)
        mixed = call(
            functools.partial(second_body, lower, half), shape(rows, HD), "vvvvv"
        )(live, oth, w_own, qkv, square)
        mixed_oth = exchanged(mixed, "tensor", 1)
        embed = call(embed_own_body, shape(rows, cols, dtype=F32), "vvvv")(
            e_mine, e_recv, mixed, combined
        )
        embed = call(embed_body, shape(rows, cols), "vvvv")(live, embed, mixed_oth, combined)
    with jax.named_scope("moments"):
        embeds = [embed] + [exchanged(embed, "dp", mask) for mask in DP_ORDER(group_count)]
        sums = ()
        for part in (embeds[:2], embeds[2:]):
            gram = call(gram_body, shape(rows, rows * len(part), dtype=F32), "v" * (1 + len(part)))(
                embed, *part
            )
            operands = (gram, exchanged(gram, "tensor", 1), *part, *sums)
            out = shape(rows, cols, dtype=F32)
            body = functools.partial(result_last_body if sums else result_body, rows * group_count)
            sums = (
                call(
                    body,
                    out,
                    "v" * len(operands),
                    copies=2 if sums else 0,
                    last=bool(sums),
                    scratch=(pltpu.VMEM(out.shape, out.dtype),) if sums else (),
                )(*operands),
            )
    return sums[0][None]


def solution(mesh):
    return jax.shard_map(
        shards,
        mesh=mesh,
        in_specs=(
            P("section", "dp", "tensor"),
            P(None, "dp"),
            P("section", None, "tensor"),
            P("section", None, "tensor"),
            P("section", None, "tensor"),
            P("section", "tensor", None),
            P("tensor", None),
        ),
        out_specs=P("section", "dp", "tensor"),
        check_vma=False,
    )
```

```python
import functools
import math

import jax
import jax.numpy as jnp
from jax import lax
from jax.experimental import pallas as pl
from jax.experimental.pallas import tpu as pltpu
from jax.sharding import PartitionSpec as P

HD = 128
QKV = 3 * HD
EPSILON = 1e-05
BF16 = jnp.bfloat16
F32 = jnp.float32
VMEM_BYTES = 18 * 1024 * 1024
SHARES = (7, 9)
WO_PARTS = 4
DP_ORDER = lambda count: reversed(range(1, count))


def shifted(value, axis, steps):
    count = lax.axis_size(axis)
    pairs = [(source, (source + steps) % count) for source in range(count)]
    return lax.ppermute(value, axis, pairs)


def exchanged(value, axis, mask):
    count = lax.axis_size(axis)
    return lax.ppermute(value, axis, [(source, source ^ mask) for source in range(count)])


def after(value, *others):
    return lax.optimization_barrier((value, *others))[0]


def dot(left, right):
    return lax.dot_general(left, right, (((1,), (0,)), ((), ())), preferred_element_type=F32)


def dot_t(left, right):
    return lax.dot_general(left, right, (((1,), (1,)), ((), ())), preferred_element_type=F32)


def shape(*dims, dtype=BF16):
    return jax.ShapeDtypeStruct(dims, dtype)


SPACES = {"s": pltpu.SMEM, "v": pltpu.VMEM, "h": pltpu.HBM}


def call(body, out_shapes, spaces, copies=0, last=False, scratch=()):
    kernel = pl.pallas_call(
        body,
        out_shape=out_shapes
        if last
        else jax.tree.map(lambda out: pltpu.VMEM(out.shape, out.dtype), out_shapes),
        in_specs=[pl.BlockSpec(memory_space=SPACES[space]) for space in spaces],
        out_specs=jax.tree.map(
            lambda _: pl.BlockSpec(memory_space=pltpu.HBM if last else pltpu.VMEM), out_shapes
        ),
        scratch_shapes=([pltpu.SemaphoreType.DMA((copies,))] if copies else []) + list(scratch),
        compiler_params=pltpu.CompilerParams(vmem_limit_bytes=VMEM_BYTES),
        cost_estimate=pl.CostEstimate(flops=0, bytes_accessed=0, transcendentals=0),
    )

    def place(operand, space):
        if space == "s":
            return operand
        return pltpu.with_memory_space_constraint(operand, SPACES[space])

    return lambda *operands: kernel(*map(place, operands, spaces))


def span(start, size):
    return pl.ds(pl.multiple_of(start, size), size)


def lane_sums(x):
    x32 = x.astype(F32)
    x2 = x32 * x32
    total = x2[:, :HD]
    for lane in range(HD, x.shape[1], HD):
        total += x2[:, lane : lane + HD]
    return total


def rms_scale(square, features):
    return lax.rsqrt(jnp.sum(square, axis=-1, keepdims=True) * (1.0 / features) + EPSILON)


def softmax_mix(qkv, live_len):
    query, key, value = (qkv[:, at : at + HD].astype(BF16) for at in range(0, QKV, HD))
    rows = query.shape[0]
    scores = dot_t(query, key) * (1.0 / math.sqrt(HD))
    key_pos = lax.broadcasted_iota(jnp.int32, (rows, rows), 1)
    scores = jnp.where(key_pos < live_len, scores, -1e30)
    weights = jnp.exp(scores - jnp.max(scores, axis=-1, keepdims=True))
    total = jnp.sum(weights, axis=-1, keepdims=True)
    return (dot(weights.astype(BF16), value) / total).astype(BF16)


def load_body(
    lens_hbm, own_hbm, wq_hbm, wk_hbm, wv_hbm, wo_hbm,
    own_ref, w_ref, qkv_ref, square_ref, live_ref, *rest,
):
    wo_own_ref, *wo_send_refs, sems, lens_ref = rest
    half = own_ref.shape[1]
    core = lax.axis_index("tensor")
    pairs = [(lens_hbm, lens_ref), (own_hbm.at[0], own_ref)]
    for side in (core, 1 - core):
        rows = span(side * half, half)
        for at, w_hbm in enumerate((wq_hbm, wk_hbm, wv_hbm)):
            pairs.append((w_hbm.at[0, rows, :], w_ref.at[rows, at * HD : (at + 1) * HD]))
    for at, ref in enumerate(wo_send_refs):
        width = ref.shape[1]
        pairs.append((wo_hbm.at[0, :, span((1 - core) * half + at * width, width)], ref))
    pairs.append((wo_hbm.at[0, :, span(core * half, half)], wo_own_ref))
    copies = [
        pltpu.make_async_copy(source, target, sems.at[index])
        for index, (source, target) in enumerate(pairs)
    ]
    for copy in copies:
        copy.start()
    copies[0].wait()
    live_ref[...] = jnp.full(live_ref.shape, lens_ref[lax.axis_index("section")], jnp.int32)
    copies[1].wait()
    own = own_ref[...]
    square_ref[...] = lane_sums(own)
    for copy in copies[2:5]:
        copy.wait()
    qkv_ref[...] = dot(own, w_ref[span(core * half, half), :])
    for copy in copies[5:]:
        copy.wait()


def first_body(live_ref, oth_ref, w_ref, qkv_ref, square_ref, *refs):
    wo_send_refs, (mixed_ref, part_ref) = refs[:-2], refs[-2:]
    half = oth_ref.shape[1]
    core = lax.axis_index("tensor")
    oth = oth_ref[...]
    qkv = qkv_ref[...] + dot(oth, w_ref[span((1 - core) * half, half), :])
    scale = rms_scale(square_ref[...] + lane_sums(oth), 2 * half)
    mixed = softmax_mix(qkv * scale, live_ref[...])
    mixed_ref[...] = mixed
    weight = jnp.concatenate([ref[...] for ref in wo_send_refs], axis=1)
    part_ref[...] = dot(mixed, weight).astype(BF16)


def held_body(own_ref, mixed_ref, wo_own_ref, *refs):
    wo_send_refs, (part_ref, held_ref) = refs[:-2], refs[-2:]
    mixed = mixed_ref[...]
    weight = jnp.concatenate([ref[...] for ref in wo_send_refs], axis=1)
    part_ref[...] = dot(mixed, weight).astype(BF16)
    held_ref[...] = own_ref[...].astype(F32) + dot(mixed, wo_own_ref[...])


def update_body(lower, held_ref, *refs):
    parts, out_ref = refs[:-1], refs[-1]
    width = out_ref.shape[1]
    part = jnp.concatenate([ref[...] for ref in parts], axis=1)
    part = part[:, part.shape[1] - width :] if len(parts) > 1 else part[:, :width]
    held = held_ref[:, lower : lower + width]
    out_ref[...] = (held + part.astype(F32)).astype(BF16)


def combine_body(lens_ref, w_own_ref, e_hbm, *refs):
    w_oth_refs, (e_ref, mine_ref, send_ref, live_ref, sems) = refs[:WO_PARTS], refs[WO_PARTS:]
    blocks = sems.shape[0]
    depth = e_ref.shape[0] // blocks
    copies = []
    for block in range(blocks):
        rows = slice(block * depth, (block + 1) * depth)
        copies.append(pltpu.make_async_copy(e_hbm.at[rows, :], e_ref.at[rows, :], sems.at[block]))
        copies[-1].start()
    cols = mine_ref.shape[1]
    core = lax.axis_index("tensor")
    w_oth = jnp.concatenate([ref[...] for ref in w_oth_refs], axis=1)
    weight = jnp.concatenate([w_own_ref[...], w_oth], axis=0)
    live_ref[...] = jnp.full(live_ref.shape, lens_ref[hop_anchor()], jnp.int32)
    for copy in copies:
        copy.wait()
    mine_ref[...] = dot(weight, e_ref[:, span(core * cols, cols)])
    send_ref[...] = dot(weight, e_ref[:, span((1 - core) * cols, cols)]).astype(BF16)


def own_body(lower, own_ref, w_ref, e_ref, *refs):
    sums, (qkv_ref, square_ref, embed_ref) = refs[:-3], refs[-3:]
    width = own_ref.shape[1]
    half = e_ref.shape[0]
    src = pl.ds(pl.multiple_of(lax.axis_index("tensor") * half + lower, HD), width)
    x = own_ref[...]
    qkv, square, embed = dot(x, w_ref[src, :]), lane_sums(x), dot(x, e_ref[lower : lower + width, :])
    if sums:
        qkv, square = qkv + sums[0][...], square + sums[1][...]
        embed = embed + sums[2][...]
    qkv_ref[...], square_ref[...], embed_ref[...] = qkv, square, embed


def own_last_body(lower, own_ref, w_ref, e_ref, sum_ref, square_in_ref, embed_in_ref, *refs):
    qkv_ref, square_ref, mine_ref, send_ref = refs
    width = own_ref.shape[1]
    half = e_ref.shape[0]
    cols = mine_ref.shape[1]
    core = lax.axis_index("tensor")
    src = pl.ds(pl.multiple_of(core * half + lower, HD), width)
    x = own_ref[...]
    for side, out_ref in ((1 - core, send_ref), (core, mine_ref)):
        at = span(side * cols, cols)
        embed = embed_in_ref[:, at] + dot(x, e_ref[lower : lower + width, at])
        out_ref[...] = embed.astype(out_ref.dtype)
    qkv_ref[...] = sum_ref[...] + dot(x, w_ref[src, :])
    square_ref[...] = square_in_ref[...] + lane_sums(x)


def other_sums(lower, half, oth_ref, w_ref):
    src = pl.ds(
        pl.multiple_of((1 - lax.axis_index("tensor")) * half + lower, HD), oth_ref.shape[1]
    )
    x = oth_ref[...]
    return dot(x, w_ref[src, :]), lane_sums(x)


def other_body(lower, half, oth_ref, w_ref, sum_ref, square_in_ref, qkv_ref, square_ref):
    qkv, square = other_sums(lower, half, oth_ref, w_ref)
    qkv_ref[...] = sum_ref[...] + qkv
    square_ref[...] = square_in_ref[...] + square


def hop_anchor():
    sections = lax.axis_size("section")
    return lax.rem(lax.axis_index("section") + sections - 1, sections)


def second_body(lower, half, live_ref, oth_ref, w_ref, sum_ref, square_in_ref, mixed_ref):
    qkv, square = other_sums(lower, half, oth_ref, w_ref)
    scale = rms_scale(square_in_ref[...] + square, 2 * half)
    mixed_ref[...] = softmax_mix((sum_ref[...] + qkv) * scale, live_ref[...])


def combine_sum_body(mine_ref, recv_ref, out_ref):
    rows = mine_ref.shape[0] // 2
    out_ref[:rows, :] = (mine_ref[:rows, :] + recv_ref[rows:, :]).astype(BF16)
    out_ref[rows:, :] = (mine_ref[rows:, :] + recv_ref[:rows, :]).astype(BF16)


def embed_own_body(mine_ref, recv_ref, mixed_ref, combined_ref, out_ref):
    product = dot(mixed_ref[...], combined_ref[: mixed_ref.shape[1], :])
    out_ref[...] = mine_ref[...] + recv_ref[...].astype(F32) + product


def embed_body(live_ref, sum_ref, mixed_ref, combined_ref, out_ref):
    embed = sum_ref[...] + dot(mixed_ref[...], combined_ref[mixed_ref.shape[1] :, :])
    live = live_ref[...]
    keep = lax.broadcasted_iota(jnp.int32, live.shape, 0) < live
    for lane in range(0, embed.shape[1], HD):
        cols = slice(lane, lane + HD)
        out_ref[:, cols] = jnp.where(keep, embed[:, cols], 0.0).astype(BF16)


def gram_body(*refs):
    own, embeds, out_ref = refs[0][...], refs[1:-1], refs[-1]
    rows = own.shape[0]
    for at, embed in enumerate(embeds):
        out_ref[:, at * rows : (at + 1) * rows] = dot_t(own, embed[...])


def result_sums(tokens, first, gram_own_ref, gram_oth_ref, embeds):
    rows = embeds[0].shape[0]
    gram = (gram_own_ref[...] + gram_oth_ref[...]) * (1.0 / tokens)
    if first:
        row = lax.broadcasted_iota(jnp.int32, gram.shape, 0)
        col = lax.broadcasted_iota(jnp.int32, gram.shape, 1)
        gram = gram - (row == col).astype(F32)
    gram = gram.astype(BF16)
    return lambda cols: dot(
        gram, jnp.concatenate([embed[:, cols] for embed in embeds], axis=0)
    )


def result_body(tokens, gram_own_ref, gram_oth_ref, *refs):
    embeds, out_ref = refs[:-1], refs[-1]
    out_ref[...] = result_sums(tokens, True, gram_own_ref, gram_oth_ref, embeds)(slice(None))


def result_last_body(tokens, gram_own_ref, gram_oth_ref, *refs):
    embeds, (sum_ref, out_hbm, sems, out_ref) = refs[:-4], refs[-4:]
    product = result_sums(tokens, False, gram_own_ref, gram_oth_ref, embeds)
    chunks = sems.shape[0]
    width = out_ref.shape[1] // chunks
    copies = []
    for chunk in range(chunks):
        cols = slice(chunk * width, (chunk + 1) * width)
        out_ref[:, cols] = sum_ref[:, cols] + product(cols)
        copies.append(
            pltpu.make_async_copy(out_ref.at[:, cols], out_hbm.at[:, cols], sems.at[chunk])
        )
        copies[-1].start()
    for copy in copies:
        copy.wait()


def shards(tokens, lengths, w_query, w_key, w_value, w_out, w_embed):
    group_count = lax.axis_size("dp")
    own_in = tokens[0]
    rows, half = own_in.shape
    features = 2 * half
    widths = [half * share // sum(SHARES) for share in SHARES]
    lowers = [sum(widths[:at]) for at in range(len(widths))]
    cols = w_embed.shape[1] // 2

    lens = lengths.reshape(-1)

    with jax.named_scope("layer_one"):
        oth = exchanged(own_in, "tensor", 1)
        own, w_own, qkv, square, live, wo_own, *wo_send = call(
            load_body,
            [
                shape(rows, half),
                shape(features, QKV),
                shape(rows, QKV, dtype=F32),
                shape(rows, HD, dtype=F32),
                shape(rows, HD, dtype=jnp.int32),
                shape(HD, half),
            ]
            + [shape(HD, half // WO_PARTS)] * WO_PARTS,
            "hhhhhh",
            9 + WO_PARTS,
            scratch=(pltpu.SMEM(lens.shape, jnp.int32),),
        )(lens, tokens, w_query, w_key, w_value, w_out)
        mixed, part = call(
            first_body, [shape(rows, HD), shape(rows, half // 2)], "v" * (5 + WO_PARTS // 2)
        )(live, oth, w_own, qkv, square, *wo_send[: WO_PARTS // 2])
        parts = [exchanged(part, "tensor", 1)]
        part, held = call(
            held_body,
            [shape(rows, half // 2), shape(rows, half, dtype=F32)],
            "v" * (3 + WO_PARTS // 2),
        )(own, mixed, wo_own, *wo_send[WO_PARTS // 2 :])
        parts.append(exchanged(part, "tensor", 1))
        state = []
        for lower, width in zip(lowers, widths):
            needed = parts if lower else parts[:1]
            body = functools.partial(update_body, lower)
            state.append(call(body, shape(rows, width), "v" * (1 + len(needed)))(held, *needed))
    with jax.named_scope("weights"):
        wo_oth = [exchanged(after(part, state[-1]), "tensor", 1) for part in wo_send]
    with jax.named_scope("hop"):
        state = [shifted(piece, "section", 1) for piece in state]
    with jax.named_scope("weights"):
        w_embed_own, c_mine, c_send, live = call(
            combine_body,
            [shape(*w_embed.shape)]
            + [shape(2 * HD, cols, dtype=F32), shape(2 * HD, cols)]
            + [shape(rows, HD, dtype=jnp.int32)],
            "svh" + "v" * WO_PARTS,
            4,
        )(lens, wo_own, w_embed, *wo_oth)
        combined = call(combine_sum_body, shape(2 * HD, cols), "vv")(
            c_mine, exchanged(c_send, "tensor", 1)
        )
    with jax.named_scope("layer_two"):
        sums = ()
        for lower, piece in zip(lowers, state):
            if sums:
                piece, combined, *sums = lax.optimization_barrier((piece, combined, *sums))
            oth = exchanged(piece, "tensor", 1)
            if lower != lowers[-1]:
                qkv, square, embed = call(
                    functools.partial(own_body, lower),
                    [shape(rows, QKV, dtype=F32), shape(rows, HD, dtype=F32), shape(rows, 2 * cols, dtype=F32)],
                    "v" * (3 + len(sums)),
                )(piece, w_own, w_embed_own, *sums)
                qkv, square = call(
                    functools.partial(other_body, lower, half),
                    [shape(rows, QKV, dtype=F32), shape(rows, HD, dtype=F32)],
                    "vvvv",
                )(oth, w_own, qkv, square)
                sums = (qkv, square, embed)
            else:
                qkv, square, e_mine, e_send = call(
                    functools.partial(own_last_body, lower),
                    [shape(rows, QKV, dtype=F32), shape(rows, HD, dtype=F32)]
                    + [shape(rows, cols, dtype=F32), shape(rows, cols)],
                    "v" * 6,
                )(piece, w_own, w_embed_own, *sums)
        e_recv = exchanged(e_send, "tensor", 1)
        mixed = call(
            functools.partial(second_body, lower, half), shape(rows, HD), "vvvvv"
        )(live, oth, w_own, qkv, square)
        mixed_oth = exchanged(mixed, "tensor", 1)
        embed = call(embed_own_body, shape(rows, cols, dtype=F32), "vvvv")(
            e_mine, e_recv, mixed, combined
        )
        embed = call(embed_body, shape(rows, cols), "vvvv")(live, embed, mixed_oth, combined)
    with jax.named_scope("moments"):
        embeds = [embed] + [exchanged(embed, "dp", mask) for mask in DP_ORDER(group_count)]
        sums = ()
        for part in (embeds[:2], embeds[2:]):
            gram = call(gram_body, shape(rows, rows * len(part), dtype=F32), "v" * (1 + len(part)))(
                embed, *part
            )
            operands = (gram, exchanged(gram, "tensor", 1), *part, *sums)
            out = shape(rows, cols, dtype=F32)
            body = functools.partial(result_last_body if sums else result_body, rows * group_count)
            sums = (
                call(
                    body,
                    out,
                    "v" * len(operands),
                    copies=2 if sums else 0,
                    last=bool(sums),
                    scratch=(pltpu.VMEM(out.shape, out.dtype),) if sums else (),
                )(*operands),
            )
    return sums[0][None]


def solution(mesh):
    return jax.shard_map(
        shards,
        mesh=mesh,
        in_specs=(
            P("section", "dp", "tensor"),
            P(None, "dp"),
            P("section", None, "tensor"),
            P("section", None, "tensor"),
            P("section", None, "tensor"),
            P("section", "tensor", None),
            P("tensor", None),
        ),
        out_specs=P("section", "dp", "tensor"),
        check_vma=False,
    )
```

```python
import functools
import math

import jax
import jax.numpy as jnp
from jax import lax
from jax.experimental import pallas as pl
from jax.experimental.pallas import tpu as pltpu
from jax.sharding import PartitionSpec as P

HD = 128
QKV = 3 * HD
EPSILON = 1e-05
BF16 = jnp.bfloat16
F32 = jnp.float32
VMEM_BYTES = 18 * 1024 * 1024
SHARES = (7, 9)
WO_PARTS = 1
DP_ORDER = lambda count: reversed(range(1, count))


def shifted(value, axis, steps):
    count = lax.axis_size(axis)
    pairs = [(source, (source + steps) % count) for source in range(count)]
    return lax.ppermute(value, axis, pairs)


def exchanged(value, axis, mask):
    count = lax.axis_size(axis)
    return lax.ppermute(value, axis, [(source, source ^ mask) for source in range(count)])


def after(value, *others):
    return lax.optimization_barrier((value, *others))[0]


def dot(left, right):
    return lax.dot_general(left, right, (((1,), (0,)), ((), ())), preferred_element_type=F32)


def dot_t(left, right):
    return lax.dot_general(left, right, (((1,), (1,)), ((), ())), preferred_element_type=F32)


def shape(*dims, dtype=BF16):
    return jax.ShapeDtypeStruct(dims, dtype)


SPACES = {"s": pltpu.SMEM, "v": pltpu.VMEM, "h": pltpu.HBM}


def call(body, out_shapes, spaces, copies=0, last=False, scratch=()):
    kernel = pl.pallas_call(
        body,
        out_shape=out_shapes
        if last
        else jax.tree.map(lambda out: pltpu.VMEM(out.shape, out.dtype), out_shapes),
        in_specs=[pl.BlockSpec(memory_space=SPACES[space]) for space in spaces],
        out_specs=jax.tree.map(
            lambda _: pl.BlockSpec(memory_space=pltpu.HBM if last else pltpu.VMEM), out_shapes
        ),
        scratch_shapes=([pltpu.SemaphoreType.DMA((copies,))] if copies else []) + list(scratch),
        compiler_params=pltpu.CompilerParams(vmem_limit_bytes=VMEM_BYTES),
        cost_estimate=pl.CostEstimate(flops=0, bytes_accessed=0, transcendentals=0),
    )

    def place(operand, space):
        if space == "s":
            return operand
        return pltpu.with_memory_space_constraint(operand, SPACES[space])

    return lambda *operands: kernel(*map(place, operands, spaces))


def span(start, size):
    return pl.ds(pl.multiple_of(start, size), size)


def lane_sums(x):
    x32 = x.astype(F32)
    x2 = x32 * x32
    total = x2[:, :HD]
    for lane in range(HD, x.shape[1], HD):
        total += x2[:, lane : lane + HD]
    return total


def rms_scale(square, features):
    return lax.rsqrt(jnp.sum(square, axis=-1, keepdims=True) * (1.0 / features) + EPSILON)


def softmax_mix(qkv, live_len):
    query, key, value = (qkv[:, at : at + HD].astype(BF16) for at in range(0, QKV, HD))
    rows = query.shape[0]
    scores = dot_t(query, key) * (1.0 / math.sqrt(HD))
    key_pos = lax.broadcasted_iota(jnp.int32, (rows, rows), 1)
    scores = jnp.where(key_pos < live_len, scores, -1e30)
    weights = jnp.exp(scores - jnp.max(scores, axis=-1, keepdims=True))
    total = jnp.sum(weights, axis=-1, keepdims=True)
    return (dot(weights.astype(BF16), value) / total).astype(BF16)


def load_body(
    lens_hbm, own_hbm, wq_hbm, wk_hbm, wv_hbm, wo_hbm,
    own_ref, w_ref, qkv_ref, square_ref, live_ref, *rest,
):
    wo_own_ref, *wo_send_refs, sems, lens_ref = rest
    half = own_ref.shape[1]
    core = lax.axis_index("tensor")
    pairs = [(lens_hbm, lens_ref), (own_hbm.at[0], own_ref)]
    for side in (core, 1 - core):
        rows = span(side * half, half)
        for at, w_hbm in enumerate((wq_hbm, wk_hbm, wv_hbm)):
            pairs.append((w_hbm.at[0, rows, :], w_ref.at[rows, at * HD : (at + 1) * HD]))
    for at, ref in enumerate(wo_send_refs):
        width = ref.shape[1]
        pairs.append((wo_hbm.at[0, :, span((1 - core) * half + at * width, width)], ref))
    pairs.append((wo_hbm.at[0, :, span(core * half, half)], wo_own_ref))
    copies = [
        pltpu.make_async_copy(source, target, sems.at[index])
        for index, (source, target) in enumerate(pairs)
    ]
    for copy in copies:
        copy.start()
    copies[0].wait()
    live_ref[...] = jnp.full(live_ref.shape, lens_ref[lax.axis_index("section")], jnp.int32)
    copies[1].wait()
    own = own_ref[...]
    square_ref[...] = lane_sums(own)
    for copy in copies[2:5]:
        copy.wait()
    qkv_ref[...] = dot(own, w_ref[span(core * half, half), :])
    for copy in copies[5:]:
        copy.wait()


def first_body(live_ref, oth_ref, w_ref, qkv_ref, square_ref, mixed_ref):
    half = oth_ref.shape[1]
    core = lax.axis_index("tensor")
    oth = oth_ref[...]
    qkv = qkv_ref[...] + dot(oth, w_ref[span((1 - core) * half, half), :])
    scale = rms_scale(square_ref[...] + lane_sums(oth), 2 * half)
    mixed_ref[...] = softmax_mix(qkv * scale, live_ref[...])


def update_body(lower, own_ref, mix_own_ref, mix_oth_ref, w_own_ref, *refs):
    w_oth_refs, out_ref = refs[:-1], refs[-1]
    cols = slice(lower, lower + out_ref.shape[1])
    w_oth = jnp.concatenate([ref[...] for ref in w_oth_refs], axis=1)
    weight = jnp.concatenate([w_own_ref[:, cols], w_oth[:, cols]], axis=0)
    mixed = jnp.concatenate([mix_own_ref[...], mix_oth_ref[...]], axis=1)
    out_ref[...] = (own_ref[:, cols].astype(F32) + dot(mixed, weight)).astype(BF16)


def combine_body(lens_ref, w_own_ref, e_hbm, *refs):
    w_oth_refs, (e_ref, mine_ref, send_ref, live_ref, sems) = refs[:WO_PARTS], refs[WO_PARTS:]
    blocks = sems.shape[0]
    depth = e_ref.shape[0] // blocks
    copies = []
    for block in range(blocks):
        rows = slice(block * depth, (block + 1) * depth)
        copies.append(pltpu.make_async_copy(e_hbm.at[rows, :], e_ref.at[rows, :], sems.at[block]))
        copies[-1].start()
    cols = mine_ref.shape[1]
    core = lax.axis_index("tensor")
    w_oth = jnp.concatenate([ref[...] for ref in w_oth_refs], axis=1)
    weight = jnp.concatenate([w_own_ref[...], w_oth], axis=0)
    live_ref[...] = jnp.full(live_ref.shape, lens_ref[hop_anchor()], jnp.int32)
    for copy in copies:
        copy.wait()
    mine_ref[...] = dot(weight, e_ref[:, span(core * cols, cols)])
    send_ref[...] = dot(weight, e_ref[:, span((1 - core) * cols, cols)]).astype(BF16)


def heads_sums(lower, half, own_side, x_ref, w_own_ref, w_oth_ref):
    core = lax.axis_index("tensor")
    side = core if own_side else 1 - core
    src = pl.ds(pl.multiple_of(side * half + lower, HD), x_ref.shape[1])
    x = x_ref[...]
    weight = jnp.concatenate([w_own_ref[src, :], w_oth_ref[src, :]], axis=1)
    return dot(x, weight), lane_sums(x)


def heads_body(lower, half, own_side, x_ref, w_own_ref, w_oth_ref, *refs):
    sums, (qkv_ref, square_ref) = refs[:-2], refs[-2:]
    qkv, square = heads_sums(lower, half, own_side, x_ref, w_own_ref, w_oth_ref)
    if sums:
        qkv, square = qkv + sums[0][...], square + sums[1][...]
    qkv_ref[...], square_ref[...] = qkv, square


def embed_piece_body(lower, x_ref, e_ref, *refs):
    embed = dot(x_ref[...], e_ref[lower : lower + x_ref.shape[1], :])
    refs[-1][...] = embed + refs[0][...] if lower else embed


def embed_last_body(lower, x_ref, e_ref, embed_ref, mine_ref, send_ref):
    cols = mine_ref.shape[1]
    core = lax.axis_index("tensor")
    x = x_ref[...]
    src = slice(lower, lower + x.shape[1])
    for side, out_ref in ((1 - core, send_ref), (core, mine_ref)):
        at = span(side * cols, cols)
        out_ref[...] = (embed_ref[:, at] + dot(x, e_ref[src, at])).astype(out_ref.dtype)


def hop_anchor():
    sections = lax.axis_size("section")
    return lax.rem(lax.axis_index("section") + sections - 1, sections)


def second_body(
    lower, half, live_ref, x_ref, w_own_ref, w_oth_ref, sum_ref, square_ref, mixed_ref
):
    qkv, square = heads_sums(lower, half, False, x_ref, w_own_ref, w_oth_ref)
    qkv = (qkv + sum_ref[...]) * rms_scale(square + square_ref[...], 2 * half)
    live = live_ref[...]
    for head in range(2):
        at = head * QKV
        mixed_ref[:, head * HD : (head + 1) * HD] = softmax_mix(qkv[:, at : at + QKV], live)


def combine_sum_body(mine_ref, recv_ref, out_ref):
    rows = mine_ref.shape[0] // 2
    out_ref[:rows, :] = (mine_ref[:rows, :] + recv_ref[rows:, :]).astype(BF16)
    out_ref[rows:, :] = (mine_ref[rows:, :] + recv_ref[:rows, :]).astype(BF16)


def embed_body(live_ref, mine_ref, recv_ref, mixed_ref, combined_ref, out_ref):
    embed = mine_ref[...] + recv_ref[...].astype(F32) + dot(mixed_ref[...], combined_ref[...])
    live = live_ref[...]
    keep = lax.broadcasted_iota(jnp.int32, live.shape, 0) < live
    for lane in range(0, embed.shape[1], HD):
        cols = slice(lane, lane + HD)
        out_ref[:, cols] = jnp.where(keep, embed[:, cols], 0.0).astype(BF16)


def gram_body(*refs):
    own, embeds, out_ref = refs[0][...], refs[1:-1], refs[-1]
    rows = own.shape[0]
    for at, embed in enumerate(embeds):
        out_ref[:, at * rows : (at + 1) * rows] = dot_t(own, embed[...])


def result_sums(tokens, first, gram_own_ref, gram_oth_ref, embeds):
    rows = embeds[0].shape[0]
    gram = (gram_own_ref[...] + gram_oth_ref[...]) * (1.0 / tokens)
    if first:
        row = lax.broadcasted_iota(jnp.int32, gram.shape, 0)
        col = lax.broadcasted_iota(jnp.int32, gram.shape, 1)
        gram = gram - (row == col).astype(F32)
    gram = gram.astype(BF16)
    return lambda cols: dot(
        gram, jnp.concatenate([embed[:, cols] for embed in embeds], axis=0)
    )


def result_body(tokens, gram_own_ref, gram_oth_ref, *refs):
    embeds, out_ref = refs[:-1], refs[-1]
    out_ref[...] = result_sums(tokens, True, gram_own_ref, gram_oth_ref, embeds)(slice(None))


def result_last_body(tokens, gram_own_ref, gram_oth_ref, *refs):
    embeds, (sum_ref, out_hbm, sems, out_ref) = refs[:-4], refs[-4:]
    product = result_sums(tokens, False, gram_own_ref, gram_oth_ref, embeds)
    chunks = sems.shape[0]
    width = out_ref.shape[1] // chunks
    copies = []
    for chunk in range(chunks):
        cols = slice(chunk * width, (chunk + 1) * width)
        out_ref[:, cols] = sum_ref[:, cols] + product(cols)
        copies.append(
            pltpu.make_async_copy(out_ref.at[:, cols], out_hbm.at[:, cols], sems.at[chunk])
        )
        copies[-1].start()
    for copy in copies:
        copy.wait()


def shards(tokens, lengths, w_query, w_key, w_value, w_out, w_embed):
    group_count = lax.axis_size("dp")
    own_in = tokens[0]
    rows, half = own_in.shape
    features = 2 * half
    widths = [half * share // sum(SHARES) for share in SHARES]
    lowers = [sum(widths[:at]) for at in range(len(widths))]
    cols = w_embed.shape[1] // 2

    lens = lengths.reshape(-1)

    with jax.named_scope("layer_one"):
        oth = exchanged(own_in, "tensor", 1)
        own, w_own, qkv, square, live, wo_own, *wo_send = call(
            load_body,
            [
                shape(rows, half),
                shape(features, QKV),
                shape(rows, QKV, dtype=F32),
                shape(rows, HD, dtype=F32),
                shape(rows, HD, dtype=jnp.int32),
                shape(HD, half),
            ]
            + [shape(HD, half // WO_PARTS)] * WO_PARTS,
            "hhhhhh",
            9 + WO_PARTS,
            scratch=(pltpu.SMEM(lens.shape, jnp.int32),),
        )(lens, tokens, w_query, w_key, w_value, w_out)
        wo_oth = [exchanged(part, "tensor", 1) for part in wo_send]
        mixed = call(first_body, shape(rows, HD), "vvvvv")(live, oth, w_own, qkv, square)
        mixed_oth = exchanged(mixed, "tensor", 1)
        state = [
            call(functools.partial(update_body, lower), shape(rows, width), "v" * (4 + WO_PARTS))(
                own, mixed, mixed_oth, wo_own, *wo_oth
            )
            for lower, width in zip(lowers, widths)
        ]
    with jax.named_scope("weights"):
        w_oth = exchanged(after(w_own, state[0]), "tensor", 1)
    with jax.named_scope("hop"):
        state = [shifted(piece, "section", 1) for piece in state]
    with jax.named_scope("weights"):
        w_embed_own, c_mine, c_send, live = call(
            combine_body,
            [shape(*w_embed.shape)]
            + [shape(2 * HD, cols, dtype=F32), shape(2 * HD, cols)]
            + [shape(rows, HD, dtype=jnp.int32)],
            "svh" + "v" * WO_PARTS,
            4,
        )(lens, wo_own, w_embed, *wo_oth)
        combined = call(combine_sum_body, shape(2 * HD, cols), "vv")(
            c_mine, exchanged(c_send, "tensor", 1)
        )
    with jax.named_scope("layer_two"):
        sums = ()
        sum_shapes = [shape(rows, 2 * QKV, dtype=F32), shape(rows, HD, dtype=F32)]
        for lower, piece in zip(lowers, state):
            if lower == lowers[-1]:
                piece, combined, embed, *sums = lax.optimization_barrier(
                    (piece, combined, embed, *sums)
                )
            oth = exchanged(piece, "tensor", 1)
            if lower != lowers[-1]:
                operands = (piece, w_embed_own, embed) if lower else (piece, w_embed_own)
                embed = call(
                    functools.partial(embed_piece_body, lower),
                    shape(rows, 2 * cols, dtype=F32),
                    "v" * len(operands),
                )(*operands)
            else:
                e_mine, e_send = call(
                    functools.partial(embed_last_body, lower),
                    [shape(rows, cols, dtype=F32), shape(rows, cols)],
                    "vvv",
                )(piece, w_embed_own, embed)
            sums = call(
                functools.partial(heads_body, lower, half, True), sum_shapes, "v" * (3 + len(sums))
            )(piece, w_own, w_oth, *sums)
            if lower != lowers[-1]:
                sums = call(
                    functools.partial(heads_body, lower, half, False), sum_shapes, "v" * 5
                )(oth, w_own, w_oth, *sums)
        e_recv = exchanged(e_send, "tensor", 1)
        mixed = call(
            functools.partial(second_body, lower, half), shape(rows, 2 * HD), "v" * 6
        )(live, oth, w_own, w_oth, *sums)
        embed = call(embed_body, shape(rows, cols), "v" * 5)(live, e_mine, e_recv, mixed, combined)
    with jax.named_scope("moments"):
        embeds = [embed] + [exchanged(embed, "dp", mask) for mask in DP_ORDER(group_count)]
        sums = ()
        for part in (embeds[:2], embeds[2:]):
            gram = call(gram_body, shape(rows, rows * len(part), dtype=F32), "v" * (1 + len(part)))(
                embed, *part
            )
            operands = (gram, exchanged(gram, "tensor", 1), *part, *sums)
            out = shape(rows, cols, dtype=F32)
            body = functools.partial(result_last_body if sums else result_body, rows * group_count)
            sums = (
                call(
                    body,
                    out,
                    "v" * len(operands),
                    copies=2 if sums else 0,
                    last=bool(sums),
                    scratch=(pltpu.VMEM(out.shape, out.dtype),) if sums else (),
                )(*operands),
            )
    return sums[0][None]


def solution(mesh):
    return jax.shard_map(
        shards,
        mesh=mesh,
        in_specs=(
            P("section", "dp", "tensor"),
            P(None, "dp"),
            P("section", None, "tensor"),
            P("section", None, "tensor"),
            P("section", None, "tensor"),
            P("section", "tensor", None),
            P("tensor", None),
        ),
        out_specs=P("section", "dp", "tensor"),
        check_vma=False,
    )
```

```python
import functools
import math

import jax
import jax.numpy as jnp
from jax import lax
from jax.experimental import pallas as pl
from jax.experimental.pallas import tpu as pltpu
from jax.sharding import PartitionSpec as P

HD = 128
QKV = 3 * HD
EPSILON = 1e-05
BF16 = jnp.bfloat16
F32 = jnp.float32
VMEM_BYTES = 18 * 1024 * 1024
SHARES = (9, 7)
WO_PARTS = 1
SWAP_CUTS = 2
DP_ORDER = lambda count: reversed(range(1, count))


def shifted(value, axis, steps):
    count = lax.axis_size(axis)
    pairs = [(source, (source + steps) % count) for source in range(count)]
    return lax.ppermute(value, axis, pairs)


def exchanged(value, axis, mask):
    count = lax.axis_size(axis)
    return lax.ppermute(value, axis, [(source, source ^ mask) for source in range(count)])


def after(value, *others):
    return lax.optimization_barrier((value, *others))[0]


def dot(left, right):
    return lax.dot_general(left, right, (((1,), (0,)), ((), ())), preferred_element_type=F32)


def dot_t(left, right):
    return lax.dot_general(left, right, (((1,), (1,)), ((), ())), preferred_element_type=F32)


def shape(*dims, dtype=BF16):
    return jax.ShapeDtypeStruct(dims, dtype)


SPACES = {"s": pltpu.SMEM, "v": pltpu.VMEM, "h": pltpu.HBM}


def call(body, out_shapes, spaces, copies=0, last=False, scratch=()):
    kernel = pl.pallas_call(
        body,
        out_shape=out_shapes
        if last
        else jax.tree.map(lambda out: pltpu.VMEM(out.shape, out.dtype), out_shapes),
        in_specs=[pl.BlockSpec(memory_space=SPACES[space]) for space in spaces],
        out_specs=jax.tree.map(
            lambda _: pl.BlockSpec(memory_space=pltpu.HBM if last else pltpu.VMEM), out_shapes
        ),
        scratch_shapes=([pltpu.SemaphoreType.DMA((copies,))] if copies else []) + list(scratch),
        compiler_params=pltpu.CompilerParams(vmem_limit_bytes=VMEM_BYTES),
        cost_estimate=pl.CostEstimate(flops=0, bytes_accessed=0, transcendentals=0),
    )

    def place(operand, space):
        if space == "s":
            return operand
        return pltpu.with_memory_space_constraint(operand, SPACES[space])

    return lambda *operands: kernel(*map(place, operands, spaces))


def span(start, size):
    return pl.ds(pl.multiple_of(start, size), size)


def lane_sums(x):
    x32 = x.astype(F32)
    x2 = x32 * x32
    total = x2[:, :HD]
    for lane in range(HD, x.shape[1], HD):
        total += x2[:, lane : lane + HD]
    return total


def rms_scale(square, features):
    return lax.rsqrt(jnp.sum(square, axis=-1, keepdims=True) * (1.0 / features) + EPSILON)


def softmax_mix(qkv, live_len):
    query, key, value = (qkv[:, at : at + HD].astype(BF16) for at in range(0, QKV, HD))
    rows = query.shape[0]
    scores = dot_t(query, key) * (1.0 / math.sqrt(HD))
    key_pos = lax.broadcasted_iota(jnp.int32, (rows, rows), 1)
    scores = jnp.where(key_pos < live_len, scores, -1e30)
    weights = jnp.exp(scores - jnp.max(scores, axis=-1, keepdims=True))
    total = jnp.sum(weights, axis=-1, keepdims=True)
    return (dot(weights.astype(BF16), value) / total).astype(BF16)


def load_body(
    lens_hbm, own_hbm, wq_hbm, wk_hbm, wv_hbm, wo_hbm,
    own_ref, w_ref, qkv_ref, square_ref, live_ref, *rest,
):
    wo_own_ref, *wo_send_refs, sems, lens_ref = rest
    half = own_ref.shape[1]
    core = lax.axis_index("tensor")
    pairs = [(lens_hbm, lens_ref), (own_hbm.at[0], own_ref)]
    for side in (core, 1 - core):
        rows = span(side * half, half)
        for at, w_hbm in enumerate((wq_hbm, wk_hbm, wv_hbm)):
            pairs.append((w_hbm.at[0, rows, :], w_ref.at[rows, at * HD : (at + 1) * HD]))
    for at, ref in enumerate(wo_send_refs):
        width = ref.shape[1]
        pairs.append((wo_hbm.at[0, :, span((1 - core) * half + at * width, width)], ref))
    pairs.append((wo_hbm.at[0, :, span(core * half, half)], wo_own_ref))
    copies = [
        pltpu.make_async_copy(source, target, sems.at[index])
        for index, (source, target) in enumerate(pairs)
    ]
    for copy in copies:
        copy.start()
    copies[0].wait()
    live_ref[...] = jnp.full(live_ref.shape, lens_ref[lax.axis_index("section")], jnp.int32)
    copies[1].wait()
    own = own_ref[...]
    square_ref[...] = lane_sums(own)
    for copy in copies[2:5]:
        copy.wait()
    qkv_ref[...] = dot(own, w_ref[span(core * half, half), :])
    for copy in copies[5:]:
        copy.wait()


def first_body(live_ref, oth_ref, w_ref, qkv_ref, square_ref, mixed_ref):
    half = oth_ref.shape[1]
    core = lax.axis_index("tensor")
    oth = oth_ref[...]
    qkv = qkv_ref[...] + dot(oth, w_ref[span((1 - core) * half, half), :])
    scale = rms_scale(square_ref[...] + lane_sums(oth), 2 * half)
    mixed_ref[...] = softmax_mix(qkv * scale, live_ref[...])


def update_body(lower, own_ref, mix_own_ref, mix_oth_ref, w_own_ref, *refs):
    w_oth_refs, out_ref = refs[:-1], refs[-1]
    cols = slice(lower, lower + out_ref.shape[1])
    w_oth = jnp.concatenate([ref[...] for ref in w_oth_refs], axis=1)
    weight = jnp.concatenate([w_own_ref[:, cols], w_oth[:, cols]], axis=0)
    mixed = jnp.concatenate([mix_own_ref[...], mix_oth_ref[...]], axis=1)
    out_ref[...] = (own_ref[:, cols].astype(F32) + dot(mixed, weight)).astype(BF16)


def combine_body(lens_ref, w_own_ref, e_hbm, *refs):
    w_oth_refs, (e_ref, mine_ref, send_ref, live_ref, sems) = refs[:WO_PARTS], refs[WO_PARTS:]
    blocks = sems.shape[0]
    depth = e_ref.shape[0] // blocks
    copies = []
    for block in range(blocks):
        rows = slice(block * depth, (block + 1) * depth)
        copies.append(pltpu.make_async_copy(e_hbm.at[rows, :], e_ref.at[rows, :], sems.at[block]))
        copies[-1].start()
    cols = mine_ref.shape[1]
    core = lax.axis_index("tensor")
    w_oth = jnp.concatenate([ref[...] for ref in w_oth_refs], axis=1)
    weight = jnp.concatenate([w_own_ref[...], w_oth], axis=0)
    live_ref[...] = jnp.full(live_ref.shape, lens_ref[hop_anchor()], jnp.int32)
    for copy in copies:
        copy.wait()
    mine_ref[...] = dot(weight, e_ref[:, span(core * cols, cols)])
    send_ref[...] = dot(weight, e_ref[:, span((1 - core) * cols, cols)]).astype(BF16)


def heads_sums(lower, half, own_side, x_refs, w_own_ref, w_oth_ref):
    core = lax.axis_index("tensor")
    side = core if own_side else 1 - core
    x = jnp.concatenate([x_ref[...] for x_ref in x_refs], axis=1)
    src = pl.ds(pl.multiple_of(side * half + lower, HD), x.shape[1])
    weight = jnp.concatenate([w_own_ref[src, :], w_oth_ref[src, :]], axis=1)
    return dot(x, weight), lane_sums(x)


def heads_body(lower, half, own_side, count, *refs):
    x_refs, (w_own_ref, w_oth_ref, *sums) = refs[:count], refs[count:-2]
    qkv_ref, square_ref = refs[-2:]
    qkv, square = heads_sums(lower, half, own_side, x_refs, w_own_ref, w_oth_ref)
    if sums:
        qkv, square = qkv + sums[0][...], square + sums[1][...]
    qkv_ref[...], square_ref[...] = qkv, square


def embed_piece_body(lower, x_ref, e_ref, *refs):
    embed = dot(x_ref[...], e_ref[lower : lower + x_ref.shape[1], :])
    refs[-1][...] = embed + refs[0][...] if lower else embed


def embed_last_body(lower, x_ref, e_ref, embed_ref, mine_ref, send_ref):
    cols = mine_ref.shape[1]
    core = lax.axis_index("tensor")
    x = x_ref[...]
    src = slice(lower, lower + x.shape[1])
    for side, out_ref in ((1 - core, send_ref), (core, mine_ref)):
        at = span(side * cols, cols)
        out_ref[...] = (embed_ref[:, at] + dot(x, e_ref[src, at])).astype(out_ref.dtype)


def hop_anchor():
    sections = lax.axis_size("section")
    return lax.rem(lax.axis_index("section") + sections - 1, sections)


def second_body(
    lower, half, live_ref, x_ref, w_own_ref, w_oth_ref, sum_ref, square_ref, mixed_ref
):
    qkv, square = heads_sums(lower, half, False, [x_ref], w_own_ref, w_oth_ref)
    qkv = (qkv + sum_ref[...]) * rms_scale(square + square_ref[...], 2 * half)
    live = live_ref[...]
    for head in range(2):
        at = head * QKV
        mixed_ref[:, head * HD : (head + 1) * HD] = softmax_mix(qkv[:, at : at + QKV], live)


def combine_sum_body(mine_ref, recv_ref, out_ref):
    rows = mine_ref.shape[0] // 2
    out_ref[:rows, :] = (mine_ref[:rows, :] + recv_ref[rows:, :]).astype(BF16)
    out_ref[rows:, :] = (mine_ref[rows:, :] + recv_ref[:rows, :]).astype(BF16)


def embed_body(live_ref, mine_ref, recv_ref, mixed_ref, combined_ref, out_ref):
    embed = mine_ref[...] + recv_ref[...].astype(F32) + dot(mixed_ref[...], combined_ref[...])
    live = live_ref[...]
    keep = lax.broadcasted_iota(jnp.int32, live.shape, 0) < live
    for lane in range(0, embed.shape[1], HD):
        cols = slice(lane, lane + HD)
        out_ref[:, cols] = jnp.where(keep, embed[:, cols], 0.0).astype(BF16)


def gram_body(*refs):
    own, embeds, out_ref = refs[0][...], refs[1:-1], refs[-1]
    rows = own.shape[0]
    for at, embed in enumerate(embeds):
        out_ref[:, at * rows : (at + 1) * rows] = dot_t(own, embed[...])


def result_sums(tokens, first, gram_own_ref, gram_oth_ref, embeds):
    rows = embeds[0].shape[0]
    gram = (gram_own_ref[...] + gram_oth_ref[...]) * (1.0 / tokens)
    if first:
        row = lax.broadcasted_iota(jnp.int32, gram.shape, 0)
        col = lax.broadcasted_iota(jnp.int32, gram.shape, 1)
        gram = gram - (row == col).astype(F32)
    gram = gram.astype(BF16)
    return lambda cols: dot(
        gram, jnp.concatenate([embed[:, cols] for embed in embeds], axis=0)
    )


def result_body(tokens, gram_own_ref, gram_oth_ref, *refs):
    embeds, out_ref = refs[:-1], refs[-1]
    out_ref[...] = result_sums(tokens, True, gram_own_ref, gram_oth_ref, embeds)(slice(None))


def result_last_body(tokens, gram_own_ref, gram_oth_ref, *refs):
    embeds, (sum_ref, out_hbm, sems, out_ref) = refs[:-4], refs[-4:]
    product = result_sums(tokens, False, gram_own_ref, gram_oth_ref, embeds)
    chunks = sems.shape[0]
    width = out_ref.shape[1] // chunks
    copies = []
    for chunk in range(chunks):
        cols = slice(chunk * width, (chunk + 1) * width)
        out_ref[:, cols] = sum_ref[:, cols] + product(cols)
        copies.append(
            pltpu.make_async_copy(out_ref.at[:, cols], out_hbm.at[:, cols], sems.at[chunk])
        )
        copies[-1].start()
    for copy in copies:
        copy.wait()


def shards(tokens, lengths, w_query, w_key, w_value, w_out, w_embed):
    group_count = lax.axis_size("dp")
    own_in = tokens[0]
    rows, half = own_in.shape
    features = 2 * half
    widths = [half * share // sum(SHARES) for share in SHARES]
    lowers = [sum(widths[:at]) for at in range(len(widths))]
    cols = w_embed.shape[1] // 2

    lens = lengths.reshape(-1)

    with jax.named_scope("layer_one"):
        oth = exchanged(own_in, "tensor", 1)
        own, w_own, qkv, square, live, wo_own, *wo_send = call(
            load_body,
            [
                shape(rows, half),
                shape(features, QKV),
                shape(rows, QKV, dtype=F32),
                shape(rows, HD, dtype=F32),
                shape(rows, HD, dtype=jnp.int32),
                shape(HD, half),
            ]
            + [shape(HD, half // WO_PARTS)] * WO_PARTS,
            "hhhhhh",
            9 + WO_PARTS,
            scratch=(pltpu.SMEM(lens.shape, jnp.int32),),
        )(lens, tokens, w_query, w_key, w_value, w_out)
        wo_oth = [exchanged(part, "tensor", 1) for part in wo_send]
        mixed = call(first_body, shape(rows, HD), "vvvvv")(live, oth, w_own, qkv, square)
        mixed_oth = exchanged(mixed, "tensor", 1)
        state = [
            call(functools.partial(update_body, lower), shape(rows, width), "v" * (4 + WO_PARTS))(
                own, mixed, mixed_oth, wo_own, *wo_oth
            )
            for lower, width in zip(lowers, widths)
        ]
    with jax.named_scope("weights"):
        w_oth = exchanged(after(w_own, state[0]), "tensor", 1)
    with jax.named_scope("hop"):
        state = [shifted(piece, "section", 1) for piece in state]
    with jax.named_scope("weights"):
        w_embed_own, c_mine, c_send, live = call(
            combine_body,
            [shape(*w_embed.shape)]
            + [shape(2 * HD, cols, dtype=F32), shape(2 * HD, cols)]
            + [shape(rows, HD, dtype=jnp.int32)],
            "svh" + "v" * WO_PARTS,
            4,
        )(lens, wo_own, w_embed, *wo_oth)
        combined = call(combine_sum_body, shape(2 * HD, cols), "vv")(
            c_mine, exchanged(c_send, "tensor", 1)
        )
    with jax.named_scope("layer_two"):
        sums = ()
        sum_shapes = [shape(rows, 2 * QKV, dtype=F32), shape(rows, HD, dtype=F32)]
        for lower, piece in zip(lowers, state):
            if lower == lowers[-1]:
                piece, combined, embed, *sums = lax.optimization_barrier(
                    (piece, combined, embed, *sums)
                )
            cuts = SWAP_CUTS if lower != lowers[-1] else 1
            step = piece.shape[1] // HD // cuts * HD
            ends = [step * at for at in range(cuts)] + [piece.shape[1]]
            oth = [
                exchanged(piece[:, start:end] if cuts > 1 else piece, "tensor", 1)
                for start, end in zip(ends, ends[1:])
            ]
            if lower != lowers[-1]:
                operands = (piece, w_embed_own, embed) if lower else (piece, w_embed_own)
                embed = call(
                    functools.partial(embed_piece_body, lower),
                    shape(rows, 2 * cols, dtype=F32),
                    "v" * len(operands),
                )(*operands)
            else:
                e_mine, e_send = call(
                    functools.partial(embed_last_body, lower),
                    [shape(rows, cols, dtype=F32), shape(rows, cols)],
                    "vvv",
                )(piece, w_embed_own, embed)
            sums = call(
                functools.partial(heads_body, lower, half, True, 1),
                sum_shapes,
                "v" * (3 + len(sums)),
            )(piece, w_own, w_oth, *sums)
            if lower != lowers[-1]:
                sums = call(
                    functools.partial(heads_body, lower, half, False, cuts),
                    sum_shapes,
                    "v" * (4 + cuts),
                )(*oth, w_own, w_oth, *sums)
        e_recv = exchanged(e_send, "tensor", 1)
        mixed = call(
            functools.partial(second_body, lower, half), shape(rows, 2 * HD), "v" * 6
        )(live, *oth, w_own, w_oth, *sums)
        embed = call(embed_body, shape(rows, cols), "v" * 5)(live, e_mine, e_recv, mixed, combined)
    with jax.named_scope("moments"):
        embeds = [embed] + [exchanged(embed, "dp", mask) for mask in DP_ORDER(group_count)]
        sums = ()
        for part in (embeds[:2], embeds[2:]):
            gram = call(gram_body, shape(rows, rows * len(part), dtype=F32), "v" * (1 + len(part)))(
                embed, *part
            )
            operands = (gram, exchanged(gram, "tensor", 1), *part, *sums)
            out = shape(rows, cols, dtype=F32)
            body = functools.partial(result_last_body if sums else result_body, rows * group_count)
            sums = (
                call(
                    body,
                    out,
                    "v" * len(operands),
                    copies=2 if sums else 0,
                    last=bool(sums),
                    scratch=(pltpu.VMEM(out.shape, out.dtype),) if sums else (),
                )(*operands),
            )
    return sums[0][None]


def solution(mesh):
    return jax.shard_map(
        shards,
        mesh=mesh,
        in_specs=(
            P("section", "dp", "tensor"),
            P(None, "dp"),
            P("section", None, "tensor"),
            P("section", None, "tensor"),
            P("section", None, "tensor"),
            P("section", "tensor", None),
            P("tensor", None),
        ),
        out_specs=P("section", "dp", "tensor"),
        check_vma=False,
    )
```

```python
import functools
import math

import jax
import jax.numpy as jnp
from jax import lax
from jax.experimental import pallas as pl
from jax.experimental.pallas import tpu as pltpu
from jax.sharding import PartitionSpec as P

HD = 128
QKV = 3 * HD
EPSILON = 1e-05
BF16 = jnp.bfloat16
F32 = jnp.float32
VMEM_BYTES = 18 * 1024 * 1024
SHARES = (9, 7)
WO_PARTS = 1
SWAP_CUTS = 2
DP_ORDER = lambda count: reversed(range(1, count))


def shifted(value, axis, steps):
    count = lax.axis_size(axis)
    pairs = [(source, (source + steps) % count) for source in range(count)]
    return lax.ppermute(value, axis, pairs)


def exchanged(value, axis, mask):
    count = lax.axis_size(axis)
    return lax.ppermute(value, axis, [(source, source ^ mask) for source in range(count)])


def after(value, *others):
    return lax.optimization_barrier((value, *others))[0]


def dot(left, right):
    return lax.dot_general(left, right, (((1,), (0,)), ((), ())), preferred_element_type=F32)


def dot_t(left, right):
    return lax.dot_general(left, right, (((1,), (1,)), ((), ())), preferred_element_type=F32)


def shape(*dims, dtype=BF16):
    return jax.ShapeDtypeStruct(dims, dtype)


SPACES = {"s": pltpu.SMEM, "v": pltpu.VMEM, "h": pltpu.HBM}


def call(body, out_shapes, spaces, copies=0, last=False, scratch=()):
    kernel = pl.pallas_call(
        body,
        out_shape=out_shapes
        if last
        else jax.tree.map(lambda out: pltpu.VMEM(out.shape, out.dtype), out_shapes),
        in_specs=[pl.BlockSpec(memory_space=SPACES[space]) for space in spaces],
        out_specs=jax.tree.map(
            lambda _: pl.BlockSpec(memory_space=pltpu.HBM if last else pltpu.VMEM), out_shapes
        ),
        scratch_shapes=([pltpu.SemaphoreType.DMA((copies,))] if copies else []) + list(scratch),
        compiler_params=pltpu.CompilerParams(vmem_limit_bytes=VMEM_BYTES),
        cost_estimate=pl.CostEstimate(flops=0, bytes_accessed=0, transcendentals=0),
    )

    def place(operand, space):
        if space == "s":
            return operand
        return pltpu.with_memory_space_constraint(operand, SPACES[space])

    return lambda *operands: kernel(*map(place, operands, spaces))


def span(start, size):
    return pl.ds(pl.multiple_of(start, size), size)


def lane_sums(x):
    x32 = x.astype(F32)
    x2 = x32 * x32
    total = x2[:, :HD]
    for lane in range(HD, x.shape[1], HD):
        total += x2[:, lane : lane + HD]
    return total


def rms_scale(square, features):
    return lax.rsqrt(jnp.sum(square, axis=-1, keepdims=True) * (1.0 / features) + EPSILON)


def softmax_mix(heads, live_len):
    parts = [[qkv[:, at : at + HD].astype(BF16) for at in range(0, QKV, HD)] for qkv in heads]
    rows = live_len.shape[0]
    scores = jnp.concatenate([dot_t(query, key) for query, key, _ in parts], axis=0)
    live = jnp.concatenate([live_len] * len(parts), axis=0)
    key_pos = lax.broadcasted_iota(jnp.int32, scores.shape, 1)
    scores = jnp.where(key_pos < live, scores * (1.0 / math.sqrt(HD)), -1e30)
    weights = jnp.exp(scores - jnp.max(scores, axis=-1, keepdims=True))
    total = jnp.sum(weights, axis=-1, keepdims=True)
    weights = weights.astype(BF16)
    mixed = [
        dot(weights[at * rows : (at + 1) * rows], value) / total[at * rows : (at + 1) * rows]
        for at, (_, _, value) in enumerate(parts)
    ]
    return jnp.concatenate(mixed, axis=1).astype(BF16)


def load_body(
    lens_hbm, own_hbm, wq_hbm, wk_hbm, wv_hbm, wo_hbm,
    own_ref, w_ref, qkv_ref, square_ref, live_ref, *rest,
):
    *wo_send_refs, sems, lens_ref = rest
    half = own_ref.shape[1]
    core = lax.axis_index("tensor")
    pairs = [(lens_hbm, lens_ref), (own_hbm.at[0], own_ref)]
    for side in (core, 1 - core):
        rows = span(side * half, half)
        for at, w_hbm in enumerate((wq_hbm, wk_hbm, wv_hbm)):
            pairs.append((w_hbm.at[0, rows, :], w_ref.at[rows, at * HD : (at + 1) * HD]))
    for at, ref in enumerate(wo_send_refs):
        width = ref.shape[1]
        pairs.append((wo_hbm.at[0, :, span((1 - core) * half + at * width, width)], ref))
    copies = [
        pltpu.make_async_copy(source, target, sems.at[index])
        for index, (source, target) in enumerate(pairs)
    ]
    for copy in copies:
        copy.start()
    copies[0].wait()
    live_ref[...] = jnp.full(live_ref.shape, lens_ref[lax.axis_index("section")], jnp.int32)
    copies[1].wait()
    own = own_ref[...]
    square_ref[...] = lane_sums(own)
    for copy in copies[2:5]:
        copy.wait()
    qkv_ref[...] = dot(own, w_ref[span(core * half, half), :])
    for copy in copies[5:]:
        copy.wait()


def first_body(live_ref, oth_ref, w_ref, qkv_ref, square_ref, mixed_ref):
    half = oth_ref.shape[1]
    core = lax.axis_index("tensor")
    oth = oth_ref[...]
    qkv = qkv_ref[...] + dot(oth, w_ref[span((1 - core) * half, half), :])
    scale = rms_scale(square_ref[...] + lane_sums(oth), 2 * half)
    mixed_ref[...] = softmax_mix([qkv * scale], live_ref[...])


def update_body(lower, own_ref, mix_own_ref, mix_oth_ref, w_own_ref, *refs):
    w_oth_refs, out_ref = refs[:-1], refs[-1]
    cols = slice(lower, lower + out_ref.shape[1])
    w_oth = jnp.concatenate([ref[...] for ref in w_oth_refs], axis=1)
    start = lax.axis_index("tensor") * own_ref.shape[1] + lower
    w_own = w_own_ref[0, :, pl.ds(pl.multiple_of(start, HD), out_ref.shape[1])]
    weight = jnp.concatenate([w_own, w_oth[:, cols]], axis=0)
    mixed = jnp.concatenate([mix_own_ref[...], mix_oth_ref[...]], axis=1)
    out_ref[...] = (own_ref[:, cols].astype(F32) + dot(mixed, weight)).astype(BF16)


def combine_body(lens_ref, w_own_ref, e_ref, *refs):
    w_oth_refs, (mine_ref, send_ref, live_ref) = refs[:WO_PARTS], refs[WO_PARTS:]
    cols = mine_ref.shape[1]
    core = lax.axis_index("tensor")
    w_oth = jnp.concatenate([ref[...] for ref in w_oth_refs], axis=1)
    half = w_oth.shape[1]
    w_own = w_own_ref[0, :, span(lax.axis_index("tensor") * half, half)]
    weight = jnp.concatenate([w_own, w_oth], axis=0)
    live_ref[...] = jnp.full(live_ref.shape, lens_ref[hop_anchor()], jnp.int32)
    mine_ref[...] = dot(weight, e_ref[:, span(core * cols, cols)])
    send_ref[...] = dot(weight, e_ref[:, span((1 - core) * cols, cols)]).astype(BF16)


def heads_sums(lower, half, own_side, x_refs, w_own_ref, w_oth_ref):
    core = lax.axis_index("tensor")
    side = core if own_side else 1 - core
    x = jnp.concatenate([x_ref[...] for x_ref in x_refs], axis=1)
    src = pl.ds(pl.multiple_of(side * half + lower, HD), x.shape[1])
    weight = jnp.concatenate([w_own_ref[src, :], w_oth_ref[src, :]], axis=1)
    return dot(x, weight), lane_sums(x)


def heads_body(lower, half, own_side, count, *refs):
    x_refs, (w_own_ref, w_oth_ref, *sums) = refs[:count], refs[count:-2]
    qkv_ref, square_ref = refs[-2:]
    qkv, square = heads_sums(lower, half, own_side, x_refs, w_own_ref, w_oth_ref)
    if sums:
        qkv, square = qkv + sums[0][...], square + sums[1][...]
    qkv_ref[...], square_ref[...] = qkv, square


def embed_piece_body(lower, x_ref, e_ref, *refs):
    embed = dot(x_ref[...], e_ref[lower : lower + x_ref.shape[1], :])
    refs[-1][...] = embed + refs[0][...] if lower else embed


def embed_last_body(lower, x_ref, e_ref, embed_ref, mine_ref, send_ref):
    cols = mine_ref.shape[1]
    core = lax.axis_index("tensor")
    x = x_ref[...]
    src = slice(lower, lower + x.shape[1])
    for side, out_ref in ((1 - core, send_ref), (core, mine_ref)):
        at = span(side * cols, cols)
        out_ref[...] = (embed_ref[:, at] + dot(x, e_ref[src, at])).astype(out_ref.dtype)


def hop_anchor():
    sections = lax.axis_size("section")
    return lax.rem(lax.axis_index("section") + sections - 1, sections)


def second_body(
    lower, half, live_ref, x_ref, w_own_ref, w_oth_ref, sum_ref, square_ref, mixed_ref
):
    qkv, square = heads_sums(lower, half, False, [x_ref], w_own_ref, w_oth_ref)
    qkv = (qkv + sum_ref[...]) * rms_scale(square + square_ref[...], 2 * half)
    mixed_ref[...] = softmax_mix([qkv[:, :QKV], qkv[:, QKV:]], live_ref[...])


def combine_sum_body(mine_ref, recv_ref, out_ref):
    rows = mine_ref.shape[0] // 2
    out_ref[:rows, :] = (mine_ref[:rows, :] + recv_ref[rows:, :]).astype(BF16)
    out_ref[rows:, :] = (mine_ref[rows:, :] + recv_ref[:rows, :]).astype(BF16)


def embed_body(live_ref, mine_ref, recv_ref, mixed_ref, combined_ref, out_ref):
    embed = mine_ref[...] + recv_ref[...].astype(F32) + dot(mixed_ref[...], combined_ref[...])
    live = live_ref[...]
    keep = lax.broadcasted_iota(jnp.int32, live.shape, 0) < live
    for lane in range(0, embed.shape[1], HD):
        cols = slice(lane, lane + HD)
        out_ref[:, cols] = jnp.where(keep, embed[:, cols], 0.0).astype(BF16)


def gram_body(*refs):
    own, embeds, out_ref = refs[0][...], refs[1:-1], refs[-1]
    rows = own.shape[0]
    for at, embed in enumerate(embeds):
        product = dot_t(own, embed[...])
        out_ref[:, at * rows : (at + 1) * rows] = product.astype(out_ref.dtype)


def result_sums(tokens, first, gram_own_ref, gram_oth_ref, embeds):
    rows = embeds[0].shape[0]
    gram = (gram_own_ref[...].astype(F32) + gram_oth_ref[...].astype(F32)) * (1.0 / tokens)
    if first:
        row = lax.broadcasted_iota(jnp.int32, gram.shape, 0)
        col = lax.broadcasted_iota(jnp.int32, gram.shape, 1)
        gram = gram - (row == col).astype(F32)
    gram = gram.astype(BF16)
    return lambda cols: dot(
        gram, jnp.concatenate([embed[:, cols] for embed in embeds], axis=0)
    )


def result_body(tokens, gram_own_ref, gram_oth_ref, *refs):
    embeds, out_ref = refs[:-1], refs[-1]
    out_ref[...] = result_sums(tokens, True, gram_own_ref, gram_oth_ref, embeds)(slice(None))


def result_last_body(tokens, gram_own_ref, gram_oth_ref, *refs):
    embeds, (sum_ref, out_hbm, sems, out_ref) = refs[:-4], refs[-4:]
    product = result_sums(tokens, False, gram_own_ref, gram_oth_ref, embeds)
    chunks = sems.shape[0]
    width = out_ref.shape[1] // chunks
    copies = []
    for chunk in range(chunks):
        cols = slice(chunk * width, (chunk + 1) * width)
        out_ref[:, cols] = sum_ref[:, cols] + product(cols)
        copies.append(
            pltpu.make_async_copy(out_ref.at[:, cols], out_hbm.at[:, cols], sems.at[chunk])
        )
        copies[-1].start()
    for copy in copies:
        copy.wait()


def shards(tokens, lengths, w_query, w_key, w_value, w_out, w_embed):
    group_count = lax.axis_size("dp")
    own_in = tokens[0]
    rows, half = own_in.shape
    features = 2 * half
    widths = [half * share // sum(SHARES) for share in SHARES]
    lowers = [sum(widths[:at]) for at in range(len(widths))]
    cols = w_embed.shape[1] // 2

    lens = lengths.reshape(-1)

    with jax.named_scope("layer_one"):
        oth = exchanged(own_in, "tensor", 1)
        own, w_own, qkv, square, live, *wo_send = call(
            load_body,
            [
                shape(rows, half),
                shape(features, QKV),
                shape(rows, QKV, dtype=F32),
                shape(rows, HD, dtype=F32),
                shape(rows, HD, dtype=jnp.int32),
            ]
            + [shape(HD, half // WO_PARTS)] * WO_PARTS,
            "hhhhhh",
            8 + WO_PARTS,
            scratch=(pltpu.SMEM(lens.shape, jnp.int32),),
        )(lens, tokens, w_query, w_key, w_value, w_out)
        wo_oth = [exchanged(part, "tensor", 1) for part in wo_send]
        mixed = call(first_body, shape(rows, HD), "vvvvv")(live, oth, w_own, qkv, square)
        mixed_oth = exchanged(mixed, "tensor", 1)
        state = [
            call(functools.partial(update_body, lower), shape(rows, width), "v" * (4 + WO_PARTS))(
                own, mixed, mixed_oth, w_out, *wo_oth
            )
            for lower, width in zip(lowers, widths)
        ]
    with jax.named_scope("weights"):
        w_oth = exchanged(after(w_own, state[0]), "tensor", 1)
    ready = state[0]
    with jax.named_scope("hop"):
        state = [shifted(piece, "section", 1) for piece in state]
    with jax.named_scope("weights"):
        w_embed_own = after(w_embed, ready)
        c_mine, c_send, live = call(
            combine_body,
            [shape(2 * HD, cols, dtype=F32), shape(2 * HD, cols)]
            + [shape(rows, HD, dtype=jnp.int32)],
            "svv" + "v" * WO_PARTS,
        )(lens, w_out, w_embed_own, *wo_oth)
        combined = call(combine_sum_body, shape(2 * HD, cols), "vv")(
            c_mine, exchanged(c_send, "tensor", 1)
        )
    with jax.named_scope("layer_two"):
        sums = ()
        sum_shapes = [shape(rows, 2 * QKV, dtype=F32), shape(rows, HD, dtype=F32)]
        for lower, piece in zip(lowers, state):
            if lower == lowers[-1]:
                piece, combined, embed, *sums = lax.optimization_barrier(
                    (piece, combined, embed, *sums)
                )
            cuts = SWAP_CUTS if lower != lowers[-1] else 1
            step = piece.shape[1] // HD // cuts * HD
            ends = [step * at for at in range(cuts)] + [piece.shape[1]]
            oth = [
                exchanged(piece[:, start:end] if cuts > 1 else piece, "tensor", 1)
                for start, end in zip(ends, ends[1:])
            ]
            if lower != lowers[-1]:
                operands = (piece, w_embed_own, embed) if lower else (piece, w_embed_own)
                embed = call(
                    functools.partial(embed_piece_body, lower),
                    shape(rows, 2 * cols, dtype=F32),
                    "v" * len(operands),
                )(*operands)
            else:
                e_mine, e_send = call(
                    functools.partial(embed_last_body, lower),
                    [shape(rows, cols, dtype=F32), shape(rows, cols)],
                    "vvv",
                )(piece, w_embed_own, embed)
            sums = call(
                functools.partial(heads_body, lower, half, True, 1),
                sum_shapes,
                "v" * (3 + len(sums)),
            )(piece, w_own, w_oth, *sums)
            if lower != lowers[-1]:
                sums = call(
                    functools.partial(heads_body, lower, half, False, cuts),
                    sum_shapes,
                    "v" * (4 + cuts),
                )(*oth, w_own, w_oth, *sums)
        e_recv = exchanged(e_send, "tensor", 1)
        mixed = call(
            functools.partial(second_body, lower, half), shape(rows, 2 * HD), "v" * 6
        )(live, *oth, w_own, w_oth, *sums)
        embed = call(embed_body, shape(rows, cols), "v" * 5)(live, e_mine, e_recv, mixed, combined)
    with jax.named_scope("moments"):
        embeds = [embed] + [exchanged(embed, "dp", mask) for mask in DP_ORDER(group_count)]
        sums = ()
        for part in (embeds[:2], embeds[2:]):
            kind = BF16 if sums else F32
            gram = call(gram_body, shape(rows, rows * len(part), dtype=kind), "v" * (1 + len(part)))(
                embed, *part
            )
            operands = (gram, exchanged(gram, "tensor", 1), *part, *sums)
            out = shape(rows, cols, dtype=F32)
            body = functools.partial(result_last_body if sums else result_body, rows * group_count)
            sums = (
                call(
                    body,
                    out,
                    "v" * len(operands),
                    copies=2 if sums else 0,
                    last=bool(sums),
                    scratch=(pltpu.VMEM(out.shape, out.dtype),) if sums else (),
                )(*operands),
            )
    return sums[0][None]


def solution(mesh):
    return jax.shard_map(
        shards,
        mesh=mesh,
        in_specs=(
            P("section", "dp", "tensor"),
            P(None, "dp"),
            P("section", None, "tensor"),
            P("section", None, "tensor"),
            P("section", None, "tensor"),
            P("section", "tensor", None),
            P("tensor", None),
        ),
        out_specs=P("section", "dp", "tensor"),
        check_vma=False,
    )
```

```python
import functools
import math

import jax
import jax.numpy as jnp
from jax import lax
from jax.experimental import pallas as pl
from jax.experimental.pallas import tpu as pltpu
from jax.sharding import PartitionSpec as P

HD = 128
QKV = 3 * HD
EPSILON = 1e-05
BF16 = jnp.bfloat16
F32 = jnp.float32
VMEM_BYTES = 18 * 1024 * 1024
SHARES = (9, 7)
WO_PARTS = 1
SWAP_CUTS = 2


def shifted(value, axis, steps):
    count = lax.axis_size(axis)
    pairs = [(source, (source + steps) % count) for source in range(count)]
    return lax.ppermute(value, axis, pairs)


def exchanged(value, axis, mask):
    count = lax.axis_size(axis)
    return lax.ppermute(value, axis, [(source, source ^ mask) for source in range(count)])


def exchanged_by_core(value, masks):
    cores = len(masks)
    count = lax.axis_size("dp") * cores
    pairs = [(source, source ^ (masks[source % cores] * cores)) for source in range(count)]
    return lax.ppermute(value, ("dp", "tensor"), pairs)


def after(value, *others):
    return lax.optimization_barrier((value, *others))[0]


def dot(left, right):
    return lax.dot_general(left, right, (((1,), (0,)), ((), ())), preferred_element_type=F32)


def dot_t(left, right):
    return lax.dot_general(left, right, (((1,), (1,)), ((), ())), preferred_element_type=F32)


def shape(*dims, dtype=BF16):
    return jax.ShapeDtypeStruct(dims, dtype)


SPACES = {"s": pltpu.SMEM, "v": pltpu.VMEM, "h": pltpu.HBM}


def call(body, out_shapes, spaces, copies=0, last=False, scratch=()):
    kernel = pl.pallas_call(
        body,
        out_shape=out_shapes
        if last
        else jax.tree.map(lambda out: pltpu.VMEM(out.shape, out.dtype), out_shapes),
        in_specs=[pl.BlockSpec(memory_space=SPACES[space]) for space in spaces],
        out_specs=jax.tree.map(
            lambda _: pl.BlockSpec(memory_space=pltpu.HBM if last else pltpu.VMEM), out_shapes
        ),
        scratch_shapes=([pltpu.SemaphoreType.DMA((copies,))] if copies else []) + list(scratch),
        compiler_params=pltpu.CompilerParams(vmem_limit_bytes=VMEM_BYTES),
        cost_estimate=pl.CostEstimate(flops=0, bytes_accessed=0, transcendentals=0),
    )

    def place(operand, space):
        if space == "s":
            return operand
        return pltpu.with_memory_space_constraint(operand, SPACES[space])

    return lambda *operands: kernel(*map(place, operands, spaces))


def span(start, size):
    return pl.ds(pl.multiple_of(start, size), size)


def lane_sums(x):
    x32 = x.astype(F32)
    x2 = x32 * x32
    total = x2[:, :HD]
    for lane in range(HD, x.shape[1], HD):
        total += x2[:, lane : lane + HD]
    return total


def rms_scale(square, features):
    return lax.rsqrt(jnp.sum(square, axis=-1, keepdims=True) * (1.0 / features) + EPSILON)


def softmax_mix(heads, live_len):
    parts = [[qkv[:, at : at + HD].astype(BF16) for at in range(0, QKV, HD)] for qkv in heads]
    rows = live_len.shape[0]
    scores = jnp.concatenate([dot_t(query, key) for query, key, _ in parts], axis=0)
    live = jnp.concatenate([live_len] * len(parts), axis=0)
    key_pos = lax.broadcasted_iota(jnp.int32, scores.shape, 1)
    scores = jnp.where(key_pos < live, scores * (1.0 / math.sqrt(HD)), -1e30)
    weights = jnp.exp(scores - jnp.max(scores, axis=-1, keepdims=True))
    total = jnp.sum(weights, axis=-1, keepdims=True)
    weights = weights.astype(BF16)
    mixed = [
        dot(weights[at * rows : (at + 1) * rows], value) / total[at * rows : (at + 1) * rows]
        for at, (_, _, value) in enumerate(parts)
    ]
    return jnp.concatenate(mixed, axis=1).astype(BF16)


def load_body(
    lens_hbm, own_hbm, wq_hbm, wk_hbm, wv_hbm, wo_hbm,
    own_ref, w_ref, qkv_ref, square_ref, live_ref, *rest,
):
    *wo_send_refs, sems, lens_ref = rest
    half = own_ref.shape[1]
    core = lax.axis_index("tensor")
    pairs = [(lens_hbm, lens_ref), (own_hbm.at[0], own_ref)]
    for side in (core, 1 - core):
        rows = span(side * half, half)
        for at, w_hbm in enumerate((wq_hbm, wk_hbm, wv_hbm)):
            pairs.append((w_hbm.at[0, rows, :], w_ref.at[rows, at * HD : (at + 1) * HD]))
    for at, ref in enumerate(wo_send_refs):
        width = ref.shape[1]
        pairs.append((wo_hbm.at[0, :, span((1 - core) * half + at * width, width)], ref))
    copies = [
        pltpu.make_async_copy(source, target, sems.at[index])
        for index, (source, target) in enumerate(pairs)
    ]
    for copy in copies:
        copy.start()
    copies[0].wait()
    live_ref[...] = jnp.full(live_ref.shape, lens_ref[lax.axis_index("section")], jnp.int32)
    copies[1].wait()
    own = own_ref[...]
    square_ref[...] = lane_sums(own)
    for copy in copies[2:5]:
        copy.wait()
    qkv_ref[...] = dot(own, w_ref[span(core * half, half), :])
    for copy in copies[5:]:
        copy.wait()


def first_body(live_ref, oth_ref, w_ref, qkv_ref, square_ref, mixed_ref):
    half = oth_ref.shape[1]
    core = lax.axis_index("tensor")
    oth = oth_ref[...]
    qkv = qkv_ref[...] + dot(oth, w_ref[span((1 - core) * half, half), :])
    scale = rms_scale(square_ref[...] + lane_sums(oth), 2 * half)
    mixed_ref[...] = softmax_mix([qkv * scale], live_ref[...])


def update_body(lower, own_ref, mix_own_ref, mix_oth_ref, w_own_ref, *refs):
    w_oth_refs, out_ref = refs[:-1], refs[-1]
    cols = slice(lower, lower + out_ref.shape[1])
    w_oth = jnp.concatenate([ref[...] for ref in w_oth_refs], axis=1)
    start = lax.axis_index("tensor") * own_ref.shape[1] + lower
    w_own = w_own_ref[0, :, pl.ds(pl.multiple_of(start, HD), out_ref.shape[1])]
    weight = jnp.concatenate([w_own, w_oth[:, cols]], axis=0)
    mixed = jnp.concatenate([mix_own_ref[...], mix_oth_ref[...]], axis=1)
    out_ref[...] = (own_ref[:, cols].astype(F32) + dot(mixed, weight)).astype(BF16)


def combine_body(lens_ref, w_own_ref, e_ref, *refs):
    w_oth_refs, (mine_ref, send_ref, live_ref) = refs[:WO_PARTS], refs[WO_PARTS:]
    cols = mine_ref.shape[1]
    core = lax.axis_index("tensor")
    w_oth = jnp.concatenate([ref[...] for ref in w_oth_refs], axis=1)
    half = w_oth.shape[1]
    w_own = w_own_ref[0, :, span(lax.axis_index("tensor") * half, half)]
    weight = jnp.concatenate([w_own, w_oth], axis=0)
    live_ref[...] = jnp.full(live_ref.shape, lens_ref[hop_anchor()], jnp.int32)
    mine_ref[...] = dot(weight, e_ref[:, span(core * cols, cols)])
    send_ref[...] = dot(weight, e_ref[:, span((1 - core) * cols, cols)]).astype(BF16)


def heads_sums(lower, half, own_side, x_refs, w_own_ref, w_oth_ref):
    core = lax.axis_index("tensor")
    side = core if own_side else 1 - core
    x = jnp.concatenate([x_ref[...] for x_ref in x_refs], axis=1)
    src = pl.ds(pl.multiple_of(side * half + lower, HD), x.shape[1])
    weight = jnp.concatenate([w_own_ref[src, :], w_oth_ref[src, :]], axis=1)
    return dot(x, weight), lane_sums(x)


def heads_body(lower, half, own_side, count, *refs):
    x_refs, (w_own_ref, w_oth_ref, *sums) = refs[:count], refs[count:-2]
    qkv_ref, square_ref = refs[-2:]
    qkv, square = heads_sums(lower, half, own_side, x_refs, w_own_ref, w_oth_ref)
    if sums:
        qkv, square = qkv + sums[0][...], square + sums[1][...]
    qkv_ref[...], square_ref[...] = qkv, square


def embed_piece_body(lower, x_ref, e_ref, *refs):
    embed = dot(x_ref[...], e_ref[lower : lower + x_ref.shape[1], :])
    refs[-1][...] = embed + refs[0][...] if lower else embed


def embed_last_body(lower, x_ref, e_ref, embed_ref, mine_ref, send_ref):
    cols = mine_ref.shape[1]
    core = lax.axis_index("tensor")
    x = x_ref[...]
    src = slice(lower, lower + x.shape[1])
    for side, out_ref in ((1 - core, send_ref), (core, mine_ref)):
        at = span(side * cols, cols)
        out_ref[...] = (embed_ref[:, at] + dot(x, e_ref[src, at])).astype(out_ref.dtype)


def hop_anchor():
    sections = lax.axis_size("section")
    return lax.rem(lax.axis_index("section") + sections - 1, sections)


def second_body(
    lower, half, live_ref, x_ref, w_own_ref, w_oth_ref, sum_ref, square_ref, mixed_ref
):
    qkv, square = heads_sums(lower, half, False, [x_ref], w_own_ref, w_oth_ref)
    qkv = (qkv + sum_ref[...]) * rms_scale(square + square_ref[...], 2 * half)
    mixed_ref[...] = softmax_mix([qkv[:, :QKV], qkv[:, QKV:]], live_ref[...])


def combine_sum_body(mine_ref, recv_ref, out_ref):
    rows = mine_ref.shape[0] // 2
    out_ref[:rows, :] = (mine_ref[:rows, :] + recv_ref[rows:, :]).astype(BF16)
    out_ref[rows:, :] = (mine_ref[rows:, :] + recv_ref[:rows, :]).astype(BF16)


def embed_body(live_ref, mine_ref, recv_ref, mixed_ref, combined_ref, out_ref):
    embed = mine_ref[...] + recv_ref[...].astype(F32) + dot(mixed_ref[...], combined_ref[...])
    live = live_ref[...]
    keep = lax.broadcasted_iota(jnp.int32, live.shape, 0) < live
    for lane in range(0, embed.shape[1], HD):
        cols = slice(lane, lane + HD)
        out_ref[:, cols] = jnp.where(keep, embed[:, cols], 0.0).astype(BF16)


def gram_body(*refs):
    own, embeds, out_ref = refs[0][...], refs[1:-1], refs[-1]
    rows = own.shape[0]
    for at, embed in enumerate(embeds):
        product = dot_t(own, embed[...])
        out_ref[:, at * rows : (at + 1) * rows] = product.astype(out_ref.dtype)


def result_sums(tokens, first, gram_own_ref, gram_oth_ref, embeds):
    rows = embeds[0].shape[0]
    gram_oth = gram_oth_ref[...].astype(F32)
    if not first:
        starts = range(0, gram_oth.shape[1], rows)
        blocks = [gram_oth[:, at : at + rows] for at in starts]
        gram_oth = jnp.concatenate(blocks[::-1], axis=1)
    gram = (gram_own_ref[...].astype(F32) + gram_oth) * (1.0 / tokens)
    if first:
        row = lax.broadcasted_iota(jnp.int32, gram.shape, 0)
        col = lax.broadcasted_iota(jnp.int32, gram.shape, 1)
        gram = gram - (row == col).astype(F32)
    gram = gram.astype(BF16)
    return lambda cols: dot(
        gram, jnp.concatenate([embed[:, cols] for embed in embeds], axis=0)
    )


def result_body(tokens, gram_own_ref, gram_oth_ref, *refs):
    embeds, out_ref = refs[:-1], refs[-1]
    out_ref[...] = result_sums(tokens, True, gram_own_ref, gram_oth_ref, embeds)(slice(None))


def result_last_body(tokens, gram_own_ref, gram_oth_ref, *refs):
    embeds, (sum_ref, out_hbm, sems, out_ref) = refs[:-4], refs[-4:]
    product = result_sums(tokens, False, gram_own_ref, gram_oth_ref, embeds)
    chunks = sems.shape[0]
    width = out_ref.shape[1] // chunks
    copies = []
    for chunk in range(chunks):
        cols = slice(chunk * width, (chunk + 1) * width)
        out_ref[:, cols] = sum_ref[:, cols] + product(cols)
        copies.append(
            pltpu.make_async_copy(out_ref.at[:, cols], out_hbm.at[:, cols], sems.at[chunk])
        )
        copies[-1].start()
    for copy in copies:
        copy.wait()


def shards(tokens, lengths, w_query, w_key, w_value, w_out, w_embed):
    group_count = lax.axis_size("dp")
    own_in = tokens[0]
    rows, half = own_in.shape
    features = 2 * half
    widths = [half * share // sum(SHARES) for share in SHARES]
    lowers = [sum(widths[:at]) for at in range(len(widths))]
    cols = w_embed.shape[1] // 2

    lens = lengths.reshape(-1)

    with jax.named_scope("layer_one"):
        oth = exchanged(own_in, "tensor", 1)
        own, w_own, qkv, square, live, *wo_send = call(
            load_body,
            [
                shape(rows, half),
                shape(features, QKV),
                shape(rows, QKV, dtype=F32),
                shape(rows, HD, dtype=F32),
                shape(rows, HD, dtype=jnp.int32),
            ]
            + [shape(HD, half // WO_PARTS)] * WO_PARTS,
            "hhhhhh",
            8 + WO_PARTS,
            scratch=(pltpu.SMEM(lens.shape, jnp.int32),),
        )(lens, tokens, w_query, w_key, w_value, w_out)
        wo_oth = [exchanged(part, "tensor", 1) for part in wo_send]
        mixed = call(first_body, shape(rows, HD), "vvvvv")(live, oth, w_own, qkv, square)
        mixed_oth = exchanged(mixed, "tensor", 1)
        state = [
            call(functools.partial(update_body, lower), shape(rows, width), "v" * (4 + WO_PARTS))(
                own, mixed, mixed_oth, w_out, *wo_oth
            )
            for lower, width in zip(lowers, widths)
        ]
    with jax.named_scope("weights"):
        w_oth = exchanged(after(w_own, state[0]), "tensor", 1)
    ready = state[0]
    with jax.named_scope("hop"):
        state = [shifted(piece, "section", 1) for piece in state]
    with jax.named_scope("weights"):
        w_embed_own = after(w_embed, ready)
        c_mine, c_send, live = call(
            combine_body,
            [shape(2 * HD, cols, dtype=F32), shape(2 * HD, cols)]
            + [shape(rows, HD, dtype=jnp.int32)],
            "svv" + "v" * WO_PARTS,
        )(lens, w_out, w_embed_own, *wo_oth)
        combined = call(combine_sum_body, shape(2 * HD, cols), "vv")(
            c_mine, exchanged(c_send, "tensor", 1)
        )
    with jax.named_scope("layer_two"):
        sums = ()
        sum_shapes = [shape(rows, 2 * QKV, dtype=F32), shape(rows, HD, dtype=F32)]
        for lower, piece in zip(lowers, state):
            if lower == lowers[-1]:
                piece, combined, embed, *sums = lax.optimization_barrier(
                    (piece, combined, embed, *sums)
                )
            cuts = SWAP_CUTS if lower != lowers[-1] else 1
            step = piece.shape[1] // HD // cuts * HD
            ends = [step * at for at in range(cuts)] + [piece.shape[1]]
            oth = [
                exchanged(piece[:, start:end] if cuts > 1 else piece, "tensor", 1)
                for start, end in zip(ends, ends[1:])
            ]
            if lower != lowers[-1]:
                operands = (piece, w_embed_own, embed) if lower else (piece, w_embed_own)
                embed = call(
                    functools.partial(embed_piece_body, lower),
                    shape(rows, 2 * cols, dtype=F32),
                    "v" * len(operands),
                )(*operands)
            else:
                e_mine, e_send = call(
                    functools.partial(embed_last_body, lower),
                    [shape(rows, cols, dtype=F32), shape(rows, cols)],
                    "vvv",
                )(piece, w_embed_own, embed)
            sums = call(
                functools.partial(heads_body, lower, half, True, 1),
                sum_shapes,
                "v" * (3 + len(sums)),
            )(piece, w_own, w_oth, *sums)
            if lower != lowers[-1]:
                sums = call(
                    functools.partial(heads_body, lower, half, False, cuts),
                    sum_shapes,
                    "v" * (4 + cuts),
                )(*oth, w_own, w_oth, *sums)
        e_recv = exchanged(e_send, "tensor", 1)
        mixed = call(
            functools.partial(second_body, lower, half), shape(rows, 2 * HD), "v" * 6
        )(live, *oth, w_own, w_oth, *sums)
        embed = call(embed_body, shape(rows, cols), "v" * 5)(live, e_mine, e_recv, mixed, combined)
    with jax.named_scope("moments"):
        first, *rest = reversed(range(1, group_count))
        embeds = [embed, exchanged(embed, "dp", first)]
        embeds += [exchanged_by_core(embed, pair) for pair in zip(rest, reversed(rest))]
        sums = ()
        for part in (embeds[:2], embeds[2:]):
            kind = BF16 if sums else F32
            gram = call(gram_body, shape(rows, rows * len(part), dtype=kind), "v" * (1 + len(part)))(
                embed, *part
            )
            operands = (gram, exchanged(gram, "tensor", 1), *part, *sums)
            out = shape(rows, cols, dtype=F32)
            body = functools.partial(result_last_body if sums else result_body, rows * group_count)
            sums = (
                call(
                    body,
                    out,
                    "v" * len(operands),
                    copies=2 if sums else 0,
                    last=bool(sums),
                    scratch=(pltpu.VMEM(out.shape, out.dtype),) if sums else (),
                )(*operands),
            )
    return sums[0][None]


def solution(mesh):
    return jax.shard_map(
        shards,
        mesh=mesh,
        in_specs=(
            P("section", "dp", "tensor"),
            P(None, "dp"),
            P("section", None, "tensor"),
            P("section", None, "tensor"),
            P("section", None, "tensor"),
            P("section", "tensor", None),
            P("tensor", None),
        ),
        out_specs=P("section", "dp", "tensor"),
        check_vma=False,
    )
```

```python
import functools
import math

import jax
import jax.numpy as jnp
from jax import lax
from jax.experimental import pallas as pl
from jax.experimental.pallas import tpu as pltpu
from jax.sharding import PartitionSpec as P

HD = 128
QKV = 3 * HD
EPSILON = 1e-05
BF16 = jnp.bfloat16
F32 = jnp.float32
VMEM_BYTES = 18 * 1024 * 1024
SHARES = (5, 5, 6)
WO_PARTS = 1
SWAP_CUTS = 1
DP_ORDER = lambda count: reversed(range(1, count))


def shifted(value, axis, steps):
    count = lax.axis_size(axis)
    pairs = [(source, (source + steps) % count) for source in range(count)]
    return lax.ppermute(value, axis, pairs)


def exchanged(value, axis, mask):
    count = lax.axis_size(axis)
    return lax.ppermute(value, axis, [(source, source ^ mask) for source in range(count)])


def after(value, *others):
    return lax.optimization_barrier((value, *others))[0]


def dot(left, right):
    return lax.dot_general(left, right, (((1,), (0,)), ((), ())), preferred_element_type=F32)


def dot_t(left, right):
    return lax.dot_general(left, right, (((1,), (1,)), ((), ())), preferred_element_type=F32)


def shape(*dims, dtype=BF16):
    return jax.ShapeDtypeStruct(dims, dtype)


SPACES = {"s": pltpu.SMEM, "v": pltpu.VMEM, "h": pltpu.HBM}


def call(body, out_shapes, spaces, copies=0, last=False, scratch=()):
    kernel = pl.pallas_call(
        body,
        out_shape=out_shapes
        if last
        else jax.tree.map(lambda out: pltpu.VMEM(out.shape, out.dtype), out_shapes),
        in_specs=[pl.BlockSpec(memory_space=SPACES[space]) for space in spaces],
        out_specs=jax.tree.map(
            lambda _: pl.BlockSpec(memory_space=pltpu.HBM if last else pltpu.VMEM), out_shapes
        ),
        scratch_shapes=([pltpu.SemaphoreType.DMA((copies,))] if copies else []) + list(scratch),
        compiler_params=pltpu.CompilerParams(vmem_limit_bytes=VMEM_BYTES),
        cost_estimate=pl.CostEstimate(flops=0, bytes_accessed=0, transcendentals=0),
    )

    def place(operand, space):
        if space == "s":
            return operand
        return pltpu.with_memory_space_constraint(operand, SPACES[space])

    return lambda *operands: kernel(*map(place, operands, spaces))


def span(start, size):
    return pl.ds(pl.multiple_of(start, size), size)


def lane_sums(x):
    x32 = x.astype(F32)
    x2 = x32 * x32
    total = x2[:, :HD]
    for lane in range(HD, x.shape[1], HD):
        total += x2[:, lane : lane + HD]
    return total


def rms_scale(square, features):
    return lax.rsqrt(jnp.sum(square, axis=-1, keepdims=True) * (1.0 / features) + EPSILON)


def softmax_mix(heads, live_len):
    parts = [[qkv[:, at : at + HD].astype(BF16) for at in range(0, QKV, HD)] for qkv in heads]
    rows = live_len.shape[0]
    scores = jnp.concatenate([dot_t(query, key) for query, key, _ in parts], axis=0)
    live = jnp.concatenate([live_len] * len(parts), axis=0)
    key_pos = lax.broadcasted_iota(jnp.int32, scores.shape, 1)
    scores = jnp.where(key_pos < live, scores * (1.0 / math.sqrt(HD)), -1e30)
    weights = jnp.exp(scores - jnp.max(scores, axis=-1, keepdims=True))
    total = jnp.sum(weights, axis=-1, keepdims=True)
    weights = weights.astype(BF16)
    mixed = [
        dot(weights[at * rows : (at + 1) * rows], value) / total[at * rows : (at + 1) * rows]
        for at, (_, _, value) in enumerate(parts)
    ]
    return jnp.concatenate(mixed, axis=1).astype(BF16)


def load_body(
    lens_hbm, own_hbm, wq_hbm, wk_hbm, wv_hbm, wo_hbm,
    own_ref, w_ref, qkv_ref, square_ref, live_ref, *rest,
):
    *wo_send_refs, sems, lens_ref = rest
    half = own_ref.shape[1]
    core = lax.axis_index("tensor")
    pairs = [(lens_hbm, lens_ref), (own_hbm.at[0], own_ref)]
    for side in (core, 1 - core):
        rows = span(side * half, half)
        for at, w_hbm in enumerate((wq_hbm, wk_hbm, wv_hbm)):
            pairs.append((w_hbm.at[0, rows, :], w_ref.at[rows, at * HD : (at + 1) * HD]))
    for at, ref in enumerate(wo_send_refs):
        width = ref.shape[1]
        pairs.append((wo_hbm.at[0, :, span((1 - core) * half + at * width, width)], ref))
    copies = [
        pltpu.make_async_copy(source, target, sems.at[index])
        for index, (source, target) in enumerate(pairs)
    ]
    for copy in copies:
        copy.start()
    copies[0].wait()
    live_ref[...] = jnp.full(live_ref.shape, lens_ref[lax.axis_index("section")], jnp.int32)
    copies[1].wait()
    own = own_ref[...]
    square_ref[...] = lane_sums(own)
    for copy in copies[2:5]:
        copy.wait()
    qkv_ref[...] = dot(own, w_ref[span(core * half, half), :])
    for copy in copies[5:]:
        copy.wait()


def first_body(live_ref, oth_ref, w_ref, qkv_ref, square_ref, mixed_ref):
    half = oth_ref.shape[1]
    core = lax.axis_index("tensor")
    oth = oth_ref[...]
    qkv = qkv_ref[...] + dot(oth, w_ref[span((1 - core) * half, half), :])
    scale = rms_scale(square_ref[...] + lane_sums(oth), 2 * half)
    mixed_ref[...] = softmax_mix([qkv * scale], live_ref[...])


def update_body(lower, own_ref, mix_own_ref, mix_oth_ref, w_own_ref, *refs):
    w_oth_refs, out_ref = refs[:-1], refs[-1]
    cols = slice(lower, lower + out_ref.shape[1])
    w_oth = jnp.concatenate([ref[...] for ref in w_oth_refs], axis=1)
    start = lax.axis_index("tensor") * own_ref.shape[1] + lower
    w_own = w_own_ref[0, :, pl.ds(pl.multiple_of(start, HD), out_ref.shape[1])]
    weight = jnp.concatenate([w_own, w_oth[:, cols]], axis=0)
    mixed = jnp.concatenate([mix_own_ref[...], mix_oth_ref[...]], axis=1)
    out_ref[...] = (own_ref[:, cols].astype(F32) + dot(mixed, weight)).astype(BF16)


def combine_body(lens_ref, w_own_ref, e_ref, *refs):
    w_oth_refs, (mine_ref, send_ref, live_ref) = refs[:WO_PARTS], refs[WO_PARTS:]
    cols = mine_ref.shape[1]
    core = lax.axis_index("tensor")
    w_oth = jnp.concatenate([ref[...] for ref in w_oth_refs], axis=1)
    half = w_oth.shape[1]
    w_own = w_own_ref[0, :, span(lax.axis_index("tensor") * half, half)]
    weight = jnp.concatenate([w_own, w_oth], axis=0)
    live_ref[...] = jnp.full(live_ref.shape, lens_ref[hop_anchor()], jnp.int32)
    mine_ref[...] = dot(weight, e_ref[:, span(core * cols, cols)])
    send_ref[...] = dot(weight, e_ref[:, span((1 - core) * cols, cols)]).astype(BF16)


def heads_sums(lower, half, own_side, x_refs, w_own_ref, w_oth_ref):
    core = lax.axis_index("tensor")
    side = core if own_side else 1 - core
    x = jnp.concatenate([x_ref[...] for x_ref in x_refs], axis=1)
    src = pl.ds(pl.multiple_of(side * half + lower, HD), x.shape[1])
    weight = jnp.concatenate([w_own_ref[src, :], w_oth_ref[src, :]], axis=1)
    return dot(x, weight), lane_sums(x)


def heads_body(lower, half, own_side, count, *refs):
    x_refs, (w_own_ref, w_oth_ref, *sums) = refs[:count], refs[count:-2]
    qkv_ref, square_ref = refs[-2:]
    qkv, square = heads_sums(lower, half, own_side, x_refs, w_own_ref, w_oth_ref)
    if sums:
        qkv, square = qkv + sums[0][...], square + sums[1][...]
    qkv_ref[...], square_ref[...] = qkv, square


def embed_piece_body(lower, x_ref, e_ref, *refs):
    embed = dot(x_ref[...], e_ref[lower : lower + x_ref.shape[1], :])
    refs[-1][...] = embed + refs[0][...] if lower else embed


def embed_last_body(lower, x_ref, e_ref, embed_ref, mine_ref, send_ref):
    cols = mine_ref.shape[1]
    core = lax.axis_index("tensor")
    x = x_ref[...]
    src = slice(lower, lower + x.shape[1])
    for side, out_ref in ((1 - core, send_ref), (core, mine_ref)):
        at = span(side * cols, cols)
        out_ref[...] = (embed_ref[:, at] + dot(x, e_ref[src, at])).astype(out_ref.dtype)


def hop_anchor():
    sections = lax.axis_size("section")
    return lax.rem(lax.axis_index("section") + sections - 1, sections)


def second_body(
    lower, half, live_ref, x_ref, w_own_ref, w_oth_ref, sum_ref, square_ref, mixed_ref
):
    qkv, square = heads_sums(lower, half, False, [x_ref], w_own_ref, w_oth_ref)
    qkv = (qkv + sum_ref[...]) * rms_scale(square + square_ref[...], 2 * half)
    mixed_ref[...] = softmax_mix([qkv[:, :QKV], qkv[:, QKV:]], live_ref[...])


def combine_sum_body(mine_ref, recv_ref, out_ref):
    rows = mine_ref.shape[0] // 2
    out_ref[:rows, :] = (mine_ref[:rows, :] + recv_ref[rows:, :]).astype(BF16)
    out_ref[rows:, :] = (mine_ref[rows:, :] + recv_ref[:rows, :]).astype(BF16)


def embed_body(live_ref, mine_ref, recv_ref, mixed_ref, combined_ref, out_ref):
    embed = mine_ref[...] + recv_ref[...].astype(F32) + dot(mixed_ref[...], combined_ref[...])
    live = live_ref[...]
    keep = lax.broadcasted_iota(jnp.int32, live.shape, 0) < live
    for lane in range(0, embed.shape[1], HD):
        cols = slice(lane, lane + HD)
        out_ref[:, cols] = jnp.where(keep, embed[:, cols], 0.0).astype(BF16)


def gram_body(*refs):
    own, embeds, out_ref = refs[0][...], refs[1:-1], refs[-1]
    rows = own.shape[0]
    for at, embed in enumerate(embeds):
        product = dot_t(own, embed[...])
        out_ref[:, at * rows : (at + 1) * rows] = product.astype(out_ref.dtype)


def result_sums(tokens, first, gram_own_ref, gram_oth_ref, embeds):
    rows = embeds[0].shape[0]
    gram = (gram_own_ref[...].astype(F32) + gram_oth_ref[...].astype(F32)) * (1.0 / tokens)
    if first:
        row = lax.broadcasted_iota(jnp.int32, gram.shape, 0)
        col = lax.broadcasted_iota(jnp.int32, gram.shape, 1)
        gram = gram - (row == col).astype(F32)
    gram = gram.astype(BF16)
    return lambda cols: dot(
        gram, jnp.concatenate([embed[:, cols] for embed in embeds], axis=0)
    )


def result_body(tokens, gram_own_ref, gram_oth_ref, *refs):
    embeds, out_ref = refs[:-1], refs[-1]
    out_ref[...] = result_sums(tokens, True, gram_own_ref, gram_oth_ref, embeds)(slice(None))


def result_last_body(tokens, gram_own_ref, gram_oth_ref, *refs):
    embeds, (sum_ref, out_hbm, sems, out_ref) = refs[:-4], refs[-4:]
    product = result_sums(tokens, False, gram_own_ref, gram_oth_ref, embeds)
    chunks = sems.shape[0]
    width = out_ref.shape[1] // chunks
    copies = []
    for chunk in range(chunks):
        cols = slice(chunk * width, (chunk + 1) * width)
        out_ref[:, cols] = sum_ref[:, cols] + product(cols)
        copies.append(
            pltpu.make_async_copy(out_ref.at[:, cols], out_hbm.at[:, cols], sems.at[chunk])
        )
        copies[-1].start()
    for copy in copies:
        copy.wait()


def shards(tokens, lengths, w_query, w_key, w_value, w_out, w_embed):
    group_count = lax.axis_size("dp")
    own_in = tokens[0]
    rows, half = own_in.shape
    features = 2 * half
    widths = [half * share // sum(SHARES) for share in SHARES]
    lowers = [sum(widths[:at]) for at in range(len(widths))]
    cols = w_embed.shape[1] // 2

    lens = lengths.reshape(-1)

    with jax.named_scope("layer_one"):
        oth = exchanged(own_in, "tensor", 1)
        own, w_own, qkv, square, live, *wo_send = call(
            load_body,
            [
                shape(rows, half),
                shape(features, QKV),
                shape(rows, QKV, dtype=F32),
                shape(rows, HD, dtype=F32),
                shape(rows, HD, dtype=jnp.int32),
            ]
            + [shape(HD, half // WO_PARTS)] * WO_PARTS,
            "hhhhhh",
            8 + WO_PARTS,
            scratch=(pltpu.SMEM(lens.shape, jnp.int32),),
        )(lens, tokens, w_query, w_key, w_value, w_out)
        wo_oth = [exchanged(part, "tensor", 1) for part in wo_send]
        mixed = call(first_body, shape(rows, HD), "vvvvv")(live, oth, w_own, qkv, square)
        mixed_oth = exchanged(mixed, "tensor", 1)
        state = [
            call(functools.partial(update_body, lower), shape(rows, width), "v" * (4 + WO_PARTS))(
                own, mixed, mixed_oth, w_out, *wo_oth
            )
            for lower, width in zip(lowers, widths)
        ]
    with jax.named_scope("weights"):
        w_oth = exchanged(after(w_own, state[0]), "tensor", 1)
    ready = state[0]
    with jax.named_scope("hop"):
        state = [shifted(piece, "section", 1) for piece in state]
    with jax.named_scope("weights"):
        w_embed_own = after(w_embed, ready)
        c_mine, c_send, live = call(
            combine_body,
            [shape(2 * HD, cols, dtype=F32), shape(2 * HD, cols)]
            + [shape(rows, HD, dtype=jnp.int32)],
            "svv" + "v" * WO_PARTS,
        )(lens, w_out, w_embed_own, *wo_oth)
        combined = call(combine_sum_body, shape(2 * HD, cols), "vv")(
            c_mine, exchanged(c_send, "tensor", 1)
        )
    with jax.named_scope("layer_two"):
        sums = ()
        sum_shapes = [shape(rows, 2 * QKV, dtype=F32), shape(rows, HD, dtype=F32)]
        for lower, piece in zip(lowers, state):
            if lower == lowers[-1]:
                piece, combined, embed, *sums = lax.optimization_barrier(
                    (piece, combined, embed, *sums)
                )
            cuts = SWAP_CUTS if lower != lowers[-1] else 1
            step = piece.shape[1] // HD // cuts * HD
            ends = [step * at for at in range(cuts)] + [piece.shape[1]]
            oth = [
                exchanged(piece[:, start:end] if cuts > 1 else piece, "tensor", 1)
                for start, end in zip(ends, ends[1:])
            ]
            if lower != lowers[-1]:
                operands = (piece, w_embed_own, embed) if lower else (piece, w_embed_own)
                embed = call(
                    functools.partial(embed_piece_body, lower),
                    shape(rows, 2 * cols, dtype=F32),
                    "v" * len(operands),
                )(*operands)
            else:
                e_mine, e_send = call(
                    functools.partial(embed_last_body, lower),
                    [shape(rows, cols, dtype=F32), shape(rows, cols)],
                    "vvv",
                )(piece, w_embed_own, embed)
            sums = call(
                functools.partial(heads_body, lower, half, True, 1),
                sum_shapes,
                "v" * (3 + len(sums)),
            )(piece, w_own, w_oth, *sums)
            if lower != lowers[-1]:
                sums = call(
                    functools.partial(heads_body, lower, half, False, cuts),
                    sum_shapes,
                    "v" * (4 + cuts),
                )(*oth, w_own, w_oth, *sums)
        e_recv = exchanged(e_send, "tensor", 1)
        mixed = call(
            functools.partial(second_body, lower, half), shape(rows, 2 * HD), "v" * 6
        )(live, *oth, w_own, w_oth, *sums)
        embed = call(embed_body, shape(rows, cols), "v" * 5)(live, e_mine, e_recv, mixed, combined)
    with jax.named_scope("moments"):
        embeds = [embed] + [exchanged(embed, "dp", mask) for mask in DP_ORDER(group_count)]
        sums = ()
        for part in (embeds[:2], embeds[2:]):
            kind = BF16 if sums else F32
            gram = call(gram_body, shape(rows, rows * len(part), dtype=kind), "v" * (1 + len(part)))(
                embed, *part
            )
            operands = (gram, exchanged(gram, "tensor", 1), *part, *sums)
            out = shape(rows, cols, dtype=F32)
            body = functools.partial(result_last_body if sums else result_body, rows * group_count)
            sums = (
                call(
                    body,
                    out,
                    "v" * len(operands),
                    copies=2 if sums else 0,
                    last=bool(sums),
                    scratch=(pltpu.VMEM(out.shape, out.dtype),) if sums else (),
                )(*operands),
            )
    return sums[0][None]


def solution(mesh):
    return jax.shard_map(
        shards,
        mesh=mesh,
        in_specs=(
            P("section", "dp", "tensor"),
            P(None, "dp"),
            P("section", None, "tensor"),
            P("section", None, "tensor"),
            P("section", None, "tensor"),
            P("section", "tensor", None),
            P("tensor", None),
        ),
        out_specs=P("section", "dp", "tensor"),
        check_vma=False,
    )
```

```python
import functools
import math

import jax
import jax.numpy as jnp
from jax import lax
from jax.experimental import pallas as pl
from jax.experimental.pallas import tpu as pltpu
from jax.sharding import PartitionSpec as P

HD = 128
QKV = 3 * HD
EPSILON = 1e-05
BF16 = jnp.bfloat16
F32 = jnp.float32
VMEM_BYTES = 18 * 1024 * 1024
SHARES = (5, 5, 6)
WO_PARTS = 1
SWAP_CUTS = 1
DP_ORDER = lambda count: reversed(range(1, count))


def shifted(value, axis, steps):
    count = lax.axis_size(axis)
    pairs = [(source, (source + steps) % count) for source in range(count)]
    return lax.ppermute(value, axis, pairs)


def exchanged(value, axis, mask):
    count = lax.axis_size(axis)
    return lax.ppermute(value, axis, [(source, source ^ mask) for source in range(count)])


def after(value, *others):
    return lax.optimization_barrier((value, *others))[0]


def dot(left, right):
    return lax.dot_general(left, right, (((1,), (0,)), ((), ())), preferred_element_type=F32)


def dot_t(left, right):
    return lax.dot_general(left, right, (((1,), (1,)), ((), ())), preferred_element_type=F32)


def shape(*dims, dtype=BF16):
    return jax.ShapeDtypeStruct(dims, dtype)


SPACES = {"s": pltpu.SMEM, "v": pltpu.VMEM, "h": pltpu.HBM}


def call(body, out_shapes, spaces, copies=0, last=False, scratch=()):
    kernel = pl.pallas_call(
        body,
        out_shape=out_shapes
        if last
        else jax.tree.map(lambda out: pltpu.VMEM(out.shape, out.dtype), out_shapes),
        in_specs=[pl.BlockSpec(memory_space=SPACES[space]) for space in spaces],
        out_specs=jax.tree.map(
            lambda _: pl.BlockSpec(memory_space=pltpu.HBM if last else pltpu.VMEM), out_shapes
        ),
        scratch_shapes=([pltpu.SemaphoreType.DMA((copies,))] if copies else []) + list(scratch),
        compiler_params=pltpu.CompilerParams(vmem_limit_bytes=VMEM_BYTES),
        cost_estimate=pl.CostEstimate(flops=0, bytes_accessed=0, transcendentals=0),
    )

    def place(operand, space):
        if space == "s":
            return operand
        return pltpu.with_memory_space_constraint(operand, SPACES[space])

    return lambda *operands: kernel(*map(place, operands, spaces))


def span(start, size):
    return pl.ds(pl.multiple_of(start, size), size)


def lane_sums(x):
    x32 = x.astype(F32)
    x2 = x32 * x32
    total = x2[:, :HD]
    for lane in range(HD, x.shape[1], HD):
        total += x2[:, lane : lane + HD]
    return total


def rms_scale(square, features):
    return lax.rsqrt(jnp.sum(square, axis=-1, keepdims=True) * (1.0 / features) + EPSILON)


def softmax_mix(heads, live_len):
    parts = [[qkv[:, at : at + HD].astype(BF16) for at in range(0, QKV, HD)] for qkv in heads]
    rows = live_len.shape[0]
    scores = jnp.concatenate([dot_t(query, key) for query, key, _ in parts], axis=0)
    live = jnp.concatenate([live_len] * len(parts), axis=0)
    key_pos = lax.broadcasted_iota(jnp.int32, scores.shape, 1)
    scores = jnp.where(key_pos < live, scores * (1.0 / math.sqrt(HD)), -1e30)
    weights = jnp.exp(scores - jnp.max(scores, axis=-1, keepdims=True))
    total = jnp.sum(weights, axis=-1, keepdims=True)
    weights = weights.astype(BF16)
    mixed = [
        dot(weights[at * rows : (at + 1) * rows], value) / total[at * rows : (at + 1) * rows]
        for at, (_, _, value) in enumerate(parts)
    ]
    return jnp.concatenate(mixed, axis=1).astype(BF16)


def load_body(
    lens_hbm, own_hbm, wq_hbm, wk_hbm, wv_hbm, wo_hbm,
    own_ref, w_ref, qkv_ref, square_ref, live_ref, *rest,
):
    *wo_send_refs, sems, lens_ref = rest
    half = own_ref.shape[1]
    core = lax.axis_index("tensor")
    pairs = [(lens_hbm, lens_ref), (own_hbm.at[0], own_ref)]
    for side in (core, 1 - core):
        rows = span(side * half, half)
        for at, w_hbm in enumerate((wq_hbm, wk_hbm, wv_hbm)):
            pairs.append((w_hbm.at[0, rows, :], w_ref.at[rows, at * HD : (at + 1) * HD]))
    for at, ref in enumerate(wo_send_refs):
        width = ref.shape[1]
        pairs.append((wo_hbm.at[0, :, span((1 - core) * half + at * width, width)], ref))
    copies = [
        pltpu.make_async_copy(source, target, sems.at[index])
        for index, (source, target) in enumerate(pairs)
    ]
    for copy in copies:
        copy.start()
    copies[0].wait()
    live_ref[...] = jnp.full(live_ref.shape, lens_ref[lax.axis_index("section")], jnp.int32)
    copies[1].wait()
    own = own_ref[...]
    square_ref[...] = lane_sums(own)
    for copy in copies[2:5]:
        copy.wait()
    qkv_ref[...] = dot(own, w_ref[span(core * half, half), :])
    for copy in copies[5:]:
        copy.wait()


def first_body(live_ref, oth_ref, w_ref, qkv_ref, square_ref, mixed_ref):
    half = oth_ref.shape[1]
    core = lax.axis_index("tensor")
    oth = oth_ref[...]
    qkv = qkv_ref[...] + dot(oth, w_ref[span((1 - core) * half, half), :])
    scale = rms_scale(square_ref[...] + lane_sums(oth), 2 * half)
    mixed_ref[...] = softmax_mix([qkv * scale], live_ref[...])


def held_body(own_ref, mixed_ref, w_ref, held_ref):
    half = own_ref.shape[1]
    weight = w_ref[0, :, span(lax.axis_index("tensor") * half, half)]
    held_ref[...] = own_ref[...].astype(F32) + dot(mixed_ref[...], weight)


def update_body(lower, held_ref, mixed_ref, *refs):
    w_refs, out_ref = refs[:-1], refs[-1]
    cols = slice(lower, lower + out_ref.shape[1])
    weight = jnp.concatenate([ref[...] for ref in w_refs], axis=1)
    out_ref[...] = (held_ref[:, cols] + dot(mixed_ref[...], weight[:, cols])).astype(BF16)


def combine_body(lens_ref, w_own_ref, e_ref, *refs):
    w_oth_refs, (mine_ref, send_ref, live_ref) = refs[:WO_PARTS], refs[WO_PARTS:]
    cols = mine_ref.shape[1]
    core = lax.axis_index("tensor")
    w_oth = jnp.concatenate([ref[...] for ref in w_oth_refs], axis=1)
    half = w_oth.shape[1]
    w_own = w_own_ref[0, :, span(lax.axis_index("tensor") * half, half)]
    weight = jnp.concatenate([w_own, w_oth], axis=0)
    live_ref[...] = jnp.full(live_ref.shape, lens_ref[hop_anchor()], jnp.int32)
    mine_ref[...] = dot(weight, e_ref[:, span(core * cols, cols)])
    send_ref[...] = dot(weight, e_ref[:, span((1 - core) * cols, cols)]).astype(BF16)


def heads_sums(lower, half, own_side, x_refs, w_own_ref, w_oth_ref):
    core = lax.axis_index("tensor")
    side = core if own_side else 1 - core
    x = jnp.concatenate([x_ref[...] for x_ref in x_refs], axis=1)
    src = pl.ds(pl.multiple_of(side * half + lower, HD), x.shape[1])
    weight = jnp.concatenate([w_own_ref[src, :], w_oth_ref[src, :]], axis=1)
    return dot(x, weight), lane_sums(x)


def heads_body(lower, half, own_side, count, *refs):
    x_refs, (w_own_ref, w_oth_ref, *sums) = refs[:count], refs[count:-2]
    qkv_ref, square_ref = refs[-2:]
    qkv, square = heads_sums(lower, half, own_side, x_refs, w_own_ref, w_oth_ref)
    if sums:
        qkv, square = qkv + sums[0][...], square + sums[1][...]
    qkv_ref[...], square_ref[...] = qkv, square


def embed_piece_body(lower, x_ref, e_ref, *refs):
    embed = dot(x_ref[...], e_ref[lower : lower + x_ref.shape[1], :])
    refs[-1][...] = embed + refs[0][...] if lower else embed


def embed_last_body(lower, x_ref, e_ref, embed_ref, mine_ref, send_ref):
    cols = mine_ref.shape[1]
    core = lax.axis_index("tensor")
    x = x_ref[...]
    src = slice(lower, lower + x.shape[1])
    for side, out_ref in ((1 - core, send_ref), (core, mine_ref)):
        at = span(side * cols, cols)
        out_ref[...] = (embed_ref[:, at] + dot(x, e_ref[src, at])).astype(out_ref.dtype)


def hop_anchor():
    sections = lax.axis_size("section")
    return lax.rem(lax.axis_index("section") + sections - 1, sections)


def second_body(
    lower, half, live_ref, x_ref, w_own_ref, w_oth_ref, sum_ref, square_ref, mixed_ref
):
    qkv, square = heads_sums(lower, half, False, [x_ref], w_own_ref, w_oth_ref)
    qkv = (qkv + sum_ref[...]) * rms_scale(square + square_ref[...], 2 * half)
    mixed_ref[...] = softmax_mix([qkv[:, :QKV], qkv[:, QKV:]], live_ref[...])


def combine_sum_body(mine_ref, recv_ref, out_ref):
    rows = mine_ref.shape[0] // 2
    out_ref[:rows, :] = (mine_ref[:rows, :] + recv_ref[rows:, :]).astype(BF16)
    out_ref[rows:, :] = (mine_ref[rows:, :] + recv_ref[:rows, :]).astype(BF16)


def embed_body(live_ref, mine_ref, recv_ref, mixed_ref, combined_ref, out_ref):
    embed = mine_ref[...] + recv_ref[...].astype(F32) + dot(mixed_ref[...], combined_ref[...])
    live = live_ref[...]
    keep = lax.broadcasted_iota(jnp.int32, live.shape, 0) < live
    for lane in range(0, embed.shape[1], HD):
        cols = slice(lane, lane + HD)
        out_ref[:, cols] = jnp.where(keep, embed[:, cols], 0.0).astype(BF16)


def gram_body(*refs):
    own, embeds, out_ref = refs[0][...], refs[1:-1], refs[-1]
    rows = own.shape[0]
    for at, embed in enumerate(embeds):
        product = dot_t(own, embed[...])
        out_ref[:, at * rows : (at + 1) * rows] = product.astype(out_ref.dtype)


def result_sums(tokens, first, gram_own_ref, gram_oth_ref, embeds):
    rows = embeds[0].shape[0]
    gram = (gram_own_ref[...].astype(F32) + gram_oth_ref[...].astype(F32)) * (1.0 / tokens)
    if first:
        row = lax.broadcasted_iota(jnp.int32, gram.shape, 0)
        col = lax.broadcasted_iota(jnp.int32, gram.shape, 1)
        gram = gram - (row == col).astype(F32)
    gram = gram.astype(BF16)
    return lambda cols: dot(
        gram, jnp.concatenate([embed[:, cols] for embed in embeds], axis=0)
    )


def result_body(tokens, gram_own_ref, gram_oth_ref, *refs):
    embeds, out_ref = refs[:-1], refs[-1]
    out_ref[...] = result_sums(tokens, True, gram_own_ref, gram_oth_ref, embeds)(slice(None))


def result_last_body(tokens, gram_own_ref, gram_oth_ref, *refs):
    embeds, (sum_ref, out_hbm, sems, out_ref) = refs[:-4], refs[-4:]
    product = result_sums(tokens, False, gram_own_ref, gram_oth_ref, embeds)
    chunks = sems.shape[0]
    width = out_ref.shape[1] // chunks
    copies = []
    for chunk in range(chunks):
        cols = slice(chunk * width, (chunk + 1) * width)
        out_ref[:, cols] = sum_ref[:, cols] + product(cols)
        copies.append(
            pltpu.make_async_copy(out_ref.at[:, cols], out_hbm.at[:, cols], sems.at[chunk])
        )
        copies[-1].start()
    for copy in copies:
        copy.wait()


def shards(tokens, lengths, w_query, w_key, w_value, w_out, w_embed):
    group_count = lax.axis_size("dp")
    own_in = tokens[0]
    rows, half = own_in.shape
    features = 2 * half
    widths = [half * share // sum(SHARES) for share in SHARES]
    lowers = [sum(widths[:at]) for at in range(len(widths))]
    cols = w_embed.shape[1] // 2

    lens = lengths.reshape(-1)

    with jax.named_scope("layer_one"):
        oth = exchanged(own_in, "tensor", 1)
        own, w_own, qkv, square, live, *wo_send = call(
            load_body,
            [
                shape(rows, half),
                shape(features, QKV),
                shape(rows, QKV, dtype=F32),
                shape(rows, HD, dtype=F32),
                shape(rows, HD, dtype=jnp.int32),
            ]
            + [shape(HD, half // WO_PARTS)] * WO_PARTS,
            "hhhhhh",
            8 + WO_PARTS,
            scratch=(pltpu.SMEM(lens.shape, jnp.int32),),
        )(lens, tokens, w_query, w_key, w_value, w_out)
        wo_oth = [exchanged(part, "tensor", 1) for part in wo_send]
        mixed = call(first_body, shape(rows, HD), "vvvvv")(live, oth, w_own, qkv, square)
        mixed_oth = exchanged(mixed, "tensor", 1)
        held = call(held_body, shape(rows, half, dtype=F32), "vvv")(own, mixed, w_out)
        state = [
            call(functools.partial(update_body, lower), shape(rows, width), "v" * (2 + WO_PARTS))(
                held, mixed_oth, *wo_oth
            )
            for lower, width in zip(lowers, widths)
        ]
    with jax.named_scope("weights"):
        w_oth = exchanged(after(w_own, state[0]), "tensor", 1)
    ready = state[0]
    with jax.named_scope("hop"):
        state = [shifted(piece, "section", 1) for piece in state]
    with jax.named_scope("weights"):
        w_embed_own = after(w_embed, ready)
        c_mine, c_send, live = call(
            combine_body,
            [shape(2 * HD, cols, dtype=F32), shape(2 * HD, cols)]
            + [shape(rows, HD, dtype=jnp.int32)],
            "svv" + "v" * WO_PARTS,
        )(lens, w_out, w_embed_own, *wo_oth)
        combined = call(combine_sum_body, shape(2 * HD, cols), "vv")(
            c_mine, exchanged(c_send, "tensor", 1)
        )
    with jax.named_scope("layer_two"):
        sums = ()
        sum_shapes = [shape(rows, 2 * QKV, dtype=F32), shape(rows, HD, dtype=F32)]
        for lower, piece in zip(lowers, state):
            if lower == lowers[-1]:
                piece, combined, embed, *sums = lax.optimization_barrier(
                    (piece, combined, embed, *sums)
                )
            cuts = SWAP_CUTS if lower != lowers[-1] else 1
            step = piece.shape[1] // HD // cuts * HD
            ends = [step * at for at in range(cuts)] + [piece.shape[1]]
            oth = [
                exchanged(piece[:, start:end] if cuts > 1 else piece, "tensor", 1)
                for start, end in zip(ends, ends[1:])
            ]
            if lower != lowers[-1]:
                operands = (piece, w_embed_own, embed) if lower else (piece, w_embed_own)
                embed = call(
                    functools.partial(embed_piece_body, lower),
                    shape(rows, 2 * cols, dtype=F32),
                    "v" * len(operands),
                )(*operands)
            else:
                e_mine, e_send = call(
                    functools.partial(embed_last_body, lower),
                    [shape(rows, cols, dtype=F32), shape(rows, cols)],
                    "vvv",
                )(piece, w_embed_own, embed)
            sums = call(
                functools.partial(heads_body, lower, half, True, 1),
                sum_shapes,
                "v" * (3 + len(sums)),
            )(piece, w_own, w_oth, *sums)
            if lower != lowers[-1]:
                sums = call(
                    functools.partial(heads_body, lower, half, False, cuts),
                    sum_shapes,
                    "v" * (4 + cuts),
                )(*oth, w_own, w_oth, *sums)
        e_recv = exchanged(e_send, "tensor", 1)
        mixed = call(
            functools.partial(second_body, lower, half), shape(rows, 2 * HD), "v" * 6
        )(live, *oth, w_own, w_oth, *sums)
        embed = call(embed_body, shape(rows, cols), "v" * 5)(live, e_mine, e_recv, mixed, combined)
    with jax.named_scope("moments"):
        embeds = [embed] + [exchanged(embed, "dp", mask) for mask in DP_ORDER(group_count)]
        sums = ()
        for part in (embeds[:2], embeds[2:]):
            kind = BF16 if sums else F32
            gram = call(gram_body, shape(rows, rows * len(part), dtype=kind), "v" * (1 + len(part)))(
                embed, *part
            )
            operands = (gram, exchanged(gram, "tensor", 1), *part, *sums)
            out = shape(rows, cols, dtype=F32)
            body = functools.partial(result_last_body if sums else result_body, rows * group_count)
            sums = (
                call(
                    body,
                    out,
                    "v" * len(operands),
                    copies=2 if sums else 0,
                    last=bool(sums),
                    scratch=(pltpu.VMEM(out.shape, out.dtype),) if sums else (),
                )(*operands),
            )
    return sums[0][None]


def solution(mesh):
    return jax.shard_map(
        shards,
        mesh=mesh,
        in_specs=(
            P("section", "dp", "tensor"),
            P(None, "dp"),
            P("section", None, "tensor"),
            P("section", None, "tensor"),
            P("section", None, "tensor"),
            P("section", "tensor", None),
            P("tensor", None),
        ),
        out_specs=P("section", "dp", "tensor"),
        check_vma=False,
    )
```
